32 devices in a mesh: groups: 2 (over x), section: 16 (over z, y, core).
Axes of the slice: x: 2, y: 2, z: 4, core: 2. Of those that a mesh axis runs over, the one named last changes fastest.
Arguments:
- hidden_in: bfloat16 [512, 3072], P(('groups', 'section')), parts along dimension 0, may hold values from -0.59765625 to 0.59765625
- latent_in: bfloat16 [512, 64], P(('groups', 'section')), parts along dimension 0, may hold values from -6 to 6
- w_qkv: bfloat16 [3, 3072, 6144], P(None, None, 'section'), may hold values from -0.109375 to 0.109375
- w_out: bfloat16 [6144, 3072], P('section'), may hold values from -0.109375 to 0.109375
- stale_kv: bfloat16 [4, 256, 6144], P('groups', None, 'section'), parts along dimension 0, may hold values from -3 to 3
- qk_gain: float32 [2, 2, 128], replicated, may hold values from 0.6 to 2.4
- block_mod: float32 [4, 3, 3072], P('groups'), parts along dimension 0, may hold values from -4 to 4
- final_mod: float32 [4, 3072], P('groups'), parts along dimension 0, may hold values from -3 to 3
- w_final: bfloat16 [3072, 64], replicated, may hold values from -0.109375 to 0.109375
- w_embed: bfloat16 [64, 3072], replicated, may hold values from -0.75 to 0.75
- patch_flow: int32 [6, 2], replicated, may hold values from 0 to 1, as said below
Outputs:
- hidden_out: bfloat16 [512, 3072], P(('groups', 'section')), parts along dimension 0
- latent_out: bfloat16 [512, 64], P(('groups', 'section')), parts along dimension 0
The draws below stay inside these ranges and needn't reach their ends.
There are 2 independent parts, one for each index of `groups`. The reference program is written for one: setup_inputs(seed, part) draws one part's arguments, and reference() takes and returns one part's arrays. A program takes and returns all parts, laid end to end along the dimension named above; an argument that names none is the same for every part. Nothing has to cross between parts.
Inputs may be any that keep to these rules, and one draw needn't show every extreme that they name: `patch_flow`: each row holds each of 0 to 1 once.
All inputs are finite; a program needn't handle non-finite values.
Results may differ from the reference program's by a relative error of at most 0.03.
Values may be sent and summed in bfloat16 or wider, within the bound.
A program may use at most 128 MiB of HBM per device.

```python
import math
import jax
import jax.numpy as jnp
from jax import lax

D = 3072
HS = 128
C = 64
HEADS = 24
TICKS = 6
PT = 128
SECTIONS = 2
TOTAL = 256


def draw_patch_flow(key, part):

    def one_row(row_index):
        return jax.random.permutation(jax.random.fold_in(key, 7001 + row_index), SECTIONS).astype(jnp.int32)
    return jax.vmap(one_row)(jnp.arange(TICKS, dtype=jnp.int32))


def draw_block_mod(key, part):
    shift_scale = jnp.clip(0.8 * jax.random.normal(jax.random.fold_in(key, 11), (SECTIONS, 2, D), jnp.float32), -3.2, 3.2)
    large_gate = jax.random.uniform(jax.random.fold_in(key, 13), (SECTIONS, D), jnp.float32, 2.5, 4.0)
    small_gate = jax.random.uniform(jax.random.fold_in(key, 17), (SECTIONS, D), jnp.float32, 0.1, 0.13)
    sign_bits = jax.random.randint(jax.random.fold_in(key, 19), (SECTIONS, D), 0, 2)
    signs = (2 * sign_bits - 1).astype(jnp.float32)
    large_count = max(D // 10, 1)

    def ranks(section_index):
        return jax.random.permutation(jax.random.fold_in(key, 5003 + section_index), D).astype(jnp.int32)
    order = jax.vmap(ranks)(jnp.arange(SECTIONS, dtype=jnp.int32))
    is_large = order < large_count
    gate = signs * jnp.where(is_large, large_gate, small_gate)
    return jnp.concatenate([shift_scale, gate[:, None, :]], axis=1).astype(jnp.float32)


def steps_of(rng, dims, cuts, low, top_value):
    loudness = 1.0
    for dim, parts in cuts:
        draws = jax.random.uniform(jax.random.fold_in(jax.random.fold_in(rng, 6), dim), (parts,), jnp.float32, low / len(cuts), top_value / len(cuts))
        loudness = loudness * jnp.repeat(jnp.exp(draws), dims[dim] // parts).reshape((-1,) + (1,) * (len(dims) - 1 - dim))
    return loudness


def scatter_about(key, extent, scale, most, shards=(), held_as=jnp.bfloat16):
    values = jax.random.normal(key, extent, jnp.float32) * scale
    if len(shards) > 0:
        values = steps_of(key, extent, shards, -0.22, 0.18) * values
    return jnp.clip(values, min=-most, max=most).astype(held_as)


def setup_inputs(seed: int = 0, part: int = 0) -> dict:
    key_of = jax.random.split(jax.random.key(seed), 12)
    part_splits = jax.random.split(jax.random.fold_in(key_of[11], part), 12)
    return {
        "hidden_in": scatter_about(part_splits[0], (TOTAL, D), 0.1, 0.59765625, ((0, 16),)),
        "latent_in": scatter_about(part_splits[1], (TOTAL, C), 1.0, 6.0, ((0, 16),)),
        "w_qkv": scatter_about(key_of[2], (3, D, SECTIONS * HEADS * HS), D ** -0.5, 0.109375, ((2, 16),)),
        "w_out": scatter_about(key_of[3], (SECTIONS * HEADS * HS, D), (HEADS * HS) ** -0.5, 0.109375, ((0, 16),)),
        "stale_kv": jnp.clip(jax.random.uniform(part_splits[4], (2, TOTAL, SECTIONS * HEADS * HS), jnp.float32, -3.0, 3.0) * steps_of(part_splits[4], (2, TOTAL, SECTIONS * HEADS * HS), ((2, 16),), -0.4, 0.0), -3.0, 3.0).astype(jnp.bfloat16),
        "qk_gain": jnp.clip(jnp.exp(jax.random.uniform(key_of[5], (SECTIONS, 2, HS), jnp.float32, math.log(0.6), math.log(2.4))), 0.6, 2.4),
        "block_mod": draw_block_mod(jax.random.fold_in(jax.random.fold_in(key_of[11], part), 71), part),
        "final_mod": scatter_about(part_splits[7], (2, D), 0.5, 3.0, (), jnp.float32),
        "w_final": scatter_about(key_of[8], (D, C), D ** -0.5, 0.109375),
        "w_embed": scatter_about(key_of[9], (C, D), C ** -0.5, 0.75),
        "patch_flow": draw_patch_flow(jax.random.fold_in(key_of[11], 71), part),
    }


def as_float(array):
    return lax.optimization_barrier(array).astype(jnp.float32)

def layer_norm(tokens, offset_row, scale_row):
    average = lax.optimization_barrier(jnp.mean(tokens, axis=-1, keepdims=True))
    centred = tokens - average
    variance = lax.optimization_barrier(jnp.mean(centred * centred, axis=-1, keepdims=True))
    return (centred * lax.rsqrt(variance + 1e-06) * (1.0 + scale_row) + offset_row).astype(jnp.bfloat16)

def head_norm(values, gain_row):
    return (values * lax.rsqrt(lax.optimization_barrier(jnp.mean(values * values, axis=-1, keepdims=True)) + 1e-06) * gain_row).astype(jnp.bfloat16)

def section_block(hidden, weights_qkv, weights_out, key_cache, value_cache, modulation, norm_gains, patch_index):
    token_count = hidden.shape[0]
    total_rows = key_cache.shape[0]
    normed = layer_norm(hidden.astype(jnp.float32), modulation[0], modulation[1])
    queries = jnp.dot(normed, weights_qkv[0], preferred_element_type=jnp.float32).reshape(token_count, HEADS, HS)
    fresh_keys = jnp.dot(normed, weights_qkv[1], preferred_element_type=jnp.float32).reshape(token_count, HEADS, HS)
    fresh_values = jnp.dot(normed, weights_qkv[2], preferred_element_type=jnp.float32)
    query_norm = head_norm(queries, norm_gains[0])
    key_norm = head_norm(fresh_keys, norm_gains[1]).reshape(token_count, HEADS * HS)
    offset = (patch_index * token_count).astype(jnp.int32)
    key_cache = lax.dynamic_update_slice(key_cache, key_norm, (offset, jnp.int32(0)))
    value_cache = lax.dynamic_update_slice(value_cache, fresh_values.astype(jnp.bfloat16), (offset, jnp.int32(0)))
    scores = jnp.einsum('qhd,khd->hqk', as_float(query_norm), as_float(key_cache).reshape(total_rows, HEADS, HS)) / math.sqrt(HS)
    exp_scores = jnp.exp(scores)
    totals = lax.optimization_barrier(jnp.sum(exp_scores, axis=-1))
    attended = jnp.einsum('hqk,khd->qhd', as_float(exp_scores.astype(jnp.bfloat16)), as_float(value_cache).reshape(total_rows, HEADS, HS))
    attended = (attended / jnp.transpose(totals)[:, :, None]).astype(jnp.bfloat16).reshape(token_count, HEADS * HS)
    projected = jnp.dot(attended, weights_out, preferred_element_type=jnp.float32)
    result = (hidden.astype(jnp.float32) + modulation[2] * projected).astype(jnp.bfloat16)
    return (result, key_cache, value_cache)

def restart(hidden, latent, final_mod, w_final, w_embed):
    normed = layer_norm(hidden.astype(jnp.float32), final_mod[0], final_mod[1])
    velocity = jnp.dot(normed, w_final, preferred_element_type=jnp.float32)
    renewed = (latent.astype(jnp.float32) + velocity).astype(jnp.bfloat16)
    embedded = jnp.dot(renewed, w_embed, preferred_element_type=jnp.float32).astype(jnp.bfloat16)
    return (embedded, renewed)

def reference(hidden_in, latent_in, w_qkv, w_out, stale_kv, qk_gain, block_mod, final_mod, w_final, w_embed, patch_flow):
    width = HEADS * HS
    hidden = hidden_in.reshape(SECTIONS, PT, D)
    latent = latent_in.reshape(SECTIONS, PT, C)
    section_qkv = jnp.transpose(w_qkv.reshape(3, D, SECTIONS, width), (2, 0, 1, 3))
    section_out = w_out.reshape(SECTIONS, width, D)
    caches = jnp.transpose(stale_kv.reshape(2, TOTAL, SECTIONS, width), (2, 0, 1, 3))
    key_cache = caches[:, 0]
    value_cache = caches[:, 1]
    block = jax.vmap(section_block)
    for tick_index in range(TICKS):
        patches = patch_flow[tick_index]
        hidden, key_cache, value_cache = block(hidden, section_qkv, section_out, key_cache, value_cache, block_mod, qk_gain, patches)
        hidden = jnp.roll(hidden, 1, axis=0)
        latent = jnp.roll(latent, 1, axis=0)
        start_hidden, start_latent = restart(hidden[0], latent[0], final_mod, w_final, w_embed)
        hidden = hidden.at[0].set(start_hidden)
        latent = latent.at[0].set(start_latent)
    return (hidden.reshape(TOTAL, D), latent.reshape(TOTAL, C))
```

```python
import functools
import math

import jax
import jax.numpy as jnp
from jax import lax
from jax.experimental import pallas as pl
from jax.experimental.pallas import tpu as pltpu
from jax.sharding import PartitionSpec as P

HS = 128
GROUP = 8
CHIPS = GROUP // 2
CHUNKS = 4
LANES = 128
EPS = 1e-06
F32 = jnp.float32
BF16 = jnp.bfloat16
MESH = pl.DeviceIdType.MESH


def wait_for(ref, sem):
    pltpu.make_async_copy(ref, ref, sem).wait()


def kernel(
    sections,
    hid, lat, wqkv, wout, kv, gain, mod, fmod, wfin, wemb, flow,
    hout, lout,
    X, Z, W, WO, KV, WE, WF, PF, SB, RB, CB, CR, OWN, R, ZS,
    load_sem, sib_sem, cross_sem, ag_sem, agsib_sem, relay_sem, z_sem, send_sem,
):
    ticks = flow.shape[0]
    rows, depth = hid.shape
    latents = lat.shape[1]
    width = wqkv.shape[2]
    total = kv.shape[1]
    tokens = rows * GROUP
    heads = width // HS
    step = depth // CHUNKS
    cols = [pl.ds(c * step, step) for c in range(CHUNKS)]

    me = lax.axis_index("section")
    sec = me // GROUP
    pos = me % GROUP
    core = pos % 2
    chip = pos // 2
    base = sec * GROUP
    sibling = base + chip * 2 + 1 - core
    low, high = chip % 2, chip // 2
    others = [chip + 1 - 2 * low, chip + 2 - 4 * high, 3 - chip]
    cross = [base + o * 2 + core for o in others]
    first = sec == 0
    last = sec == sections - 1
    after = (me + GROUP) % (sections * GROUP)
    before = (me + (sections - 1) * GROUP) % (sections * GROUP)
    last_base = (sections - 1) * GROUP

    def remote(src, dst, send, recv, target):
        return pltpu.make_async_remote_copy(
            src_ref=src, dst_ref=dst, send_sem=send, recv_sem=recv,
            device_id={"section": target}, device_id_type=MESH,
        )

    loads = [
        pltpu.make_async_copy(hid, X.at[0, pos], load_sem.at[0]),
        pltpu.make_async_copy(wqkv.at[0], W.at[:, pl.ds(0, width)], load_sem.at[1]),
        pltpu.make_async_copy(wqkv.at[1], W.at[:, pl.ds(width, width)], load_sem.at[2]),
        pltpu.make_async_copy(wqkv.at[2], W.at[:, pl.ds(2 * width, width)], load_sem.at[3]),
        pltpu.make_async_copy(kv, KV, load_sem.at[4]),
        pltpu.make_async_copy(wout, WO, load_sem.at[5]),
        pltpu.make_async_copy(wemb, WE, load_sem.at[6]),
        pltpu.make_async_copy(wfin, WF, load_sem.at[7]),
    ]
    for load in loads:
        load.start()

    barrier = pltpu.get_barrier_semaphore()

    def greet(target):
        pl.semaphore_signal(barrier, inc=1, device_id={"section": target}, device_id_type=MESH)

    greet(sibling)
    for target in cross:
        greet(target)

    @pl.when(first)
    def _():
        for i in range(GROUP):
            greet(last_base + i)

    @pl.when(last)
    def _():
        for i in range(GROUP):
            greet(i)

    if sections > 2:

        @pl.when(jnp.logical_not(last))
        def _():
            greet(after)

        @pl.when(jnp.logical_not(first))
        def _():
            greet(before)

    if sections == 2:
        pl.semaphore_wait(barrier, CHIPS + GROUP)
    else:
        edge = jnp.logical_or(first, last)

        @pl.when(edge)
        def _():
            pl.semaphore_wait(barrier, CHIPS + GROUP + 1)

        @pl.when(jnp.logical_not(edge))
        def _():
            pl.semaphore_wait(barrier, CHIPS + 2)

    ZS[...] = jnp.zeros_like(ZS)
    Z[0, pos] = jnp.zeros((rows, LANES), BF16)
    Z[0, pos, :, 0:latents] = lat[...]
    loads[0].wait()

    def embed(z, c):
        return jnp.dot(z, WE[:, cols[c]], preferred_element_type=F32).astype(BF16)

    def gather(t):
        def forward(c):
            wait_for(X.at[t, pl.ds(0, 3), :, cols[c]], ag_sem.at[c])
            for o in others:
                block = X.at[t, o * 2 + core, :, cols[c]]
                remote(block, block, send_sem.at[0], agsib_sem, sibling).start()

        for c in range(CHUNKS):

            @pl.when(t > 0)
            def _():
                wait_for(X.at[t, pos, :, cols[c]], relay_sem.at[t, c])

            block = X.at[t, pos, :, cols[c]]
            for target in cross:
                remote(block, block, send_sem.at[0], ag_sem.at[c], target).start()
            remote(block, block, send_sem.at[0], agsib_sem, sibling).start()
            if c > 0:
                forward(c - 1)
        forward(CHUNKS - 1)
        wait_for(X.at[t, pl.ds(0, CHIPS)], agsib_sem)
        wait_for(X.at[t, pl.ds(0, GROUP - 1)], send_sem.at[0])

    def tick(t, carry):
        par = t % 2

        @pl.when(jnp.logical_and(t > 0, first))
        def _():
            wait_for(Z.at[t], z_sem.at[t])
            z = Z[t].reshape(tokens, LANES)[:, :latents]
            for c in range(CHUNKS):
                X[t, :, :, cols[c]] = embed(z, c).reshape(GROUP, rows, step)

        @pl.when(jnp.logical_and(t > 0, jnp.logical_not(first)))
        def _():
            wait_for(Z.at[t, pos], z_sem.at[t])

        @pl.when(jnp.logical_or(t == 0, jnp.logical_not(first)))
        def _():
            gather(t)

        @pl.when(t == 0)
        def _():
            for load in loads[1:]:
                load.wait()

        def part(c):
            return X[t, :, :, cols[c]].reshape(tokens, step).astype(F32)

        mean = sum(jnp.sum(part(c), axis=-1, keepdims=True) for c in range(CHUNKS)) / depth
        variance = (
            sum(
                jnp.sum(jnp.square(part(c) - mean), axis=-1, keepdims=True) for c in range(CHUNKS)
            )
            / depth
        )
        inverse = lax.rsqrt(variance + EPS)
        qkv = None
        for c in range(CHUNKS):
            normed = (
                (part(c) - mean) * inverse * (1.0 + mod[sec, 1:2, cols[c]])
                + mod[sec, 0:1, cols[c]]
            ).astype(BF16)
            term = jnp.dot(normed, W[cols[c], :], preferred_element_type=F32)
            qkv = term if qkv is None else qkv + term

        def head_norm(v, g):
            return (
                v * lax.rsqrt(jnp.mean(v * v, axis=-1, keepdims=True) + EPS) * g
            ).astype(BF16)

        patch = flow[t, sec]
        outs = []
        for h in range(heads):
            at = slice(h * HS, (h + 1) * HS)
            qn = head_norm(qkv[:, at], gain[sec, 0:1, :])
            kn = head_norm(qkv[:, width + h * HS : width + (h + 1) * HS], gain[sec, 1:2, :])
            vb = qkv[:, 2 * width + h * HS : 2 * width + (h + 1) * HS].astype(BF16)
            for which, fresh in ((0, kn), (1, vb)):
                for j in range(total // tokens):
                    place = slice(j * tokens, (j + 1) * tokens)
                    KV[which, place, at] = jnp.where(
                        patch == j, fresh.astype(F32), KV[which, place, at].astype(F32)
                    ).astype(BF16)
            scores = lax.dot_general(
                qn, KV[0, :, at], (((1,), (1,)), ((), ())), preferred_element_type=F32
            ) * (1.0 / math.sqrt(HS))
            e = jnp.exp(scores)
            totals = jnp.sum(e, axis=-1, keepdims=True)
            mixed = jnp.dot(e.astype(BF16), KV[1, :, at], preferred_element_type=F32)
            outs.append((mixed / totals).astype(BF16))
        attended = jnp.concatenate(outs, axis=1)

        for c in range(CHUNKS):
            product = jnp.dot(attended, WO[:, cols[c]], preferred_element_type=F32)
            product = product.reshape(CHIPS, 2, rows, step)
            for side in range(2):
                PF[side, :, :, cols[c]] = product[:, side]
            SB[:, :, cols[c]] = PF[1 - core, :, :, cols[c]].astype(BF16)
            remote(
                SB.at[:, :, cols[c]], RB.at[par, :, :, cols[c]],
                send_sem.at[1], sib_sem.at[par, c], sibling,
            ).start()

        for c in range(CHUNKS):
            wait_for(RB.at[par, :, :, cols[c]], sib_sem.at[par, c])
            both = PF[core, :, :, cols[c]] + RB[par, :, :, cols[c]].astype(F32)
            PF[core, :, :, cols[c]] = both
            CB[:, :, cols[c]] = both.astype(BF16)
            for r in range(CHIPS - 1):
                remote(
                    CB.at[others[r], :, cols[c]], CR.at[par, r, :, cols[c]],
                    send_sem.at[2], cross_sem.at[par, c], cross[r],
                ).start()

        for c in range(CHUNKS):
            wait_for(CR.at[par, :, :, cols[c]], cross_sem.at[par, c])
            summed = PF[core, chip, :, cols[c]]
            for r in range(CHIPS - 1):
                summed = summed + CR[par, r, :, cols[c]].astype(F32)
            result = X[t, pos, :, cols[c]].astype(F32) + mod[sec, 2:3, cols[c]] * summed
            R[:, cols[c]] = result.astype(BF16)

            @pl.when(jnp.logical_not(last))
            def _():
                remote(
                    R.at[:, cols[c]], X.at[t + 1, pos, :, cols[c]],
                    send_sem.at[3], relay_sem.at[t + 1, c], after,
                ).start()

        @pl.when(jnp.logical_not(last))
        def _():
            copy = remote(Z.at[t, pos], Z.at[t + 1, pos], send_sem.at[4], z_sem.at[t + 1], after)
            copy.start()
            wait_for(Z.at[t, pos], send_sem.at[4])
            wait_for(R, send_sem.at[3])

        @pl.when(last)
        def _():
            x = R[...].astype(F32)
            centred = x - jnp.mean(x, axis=-1, keepdims=True)
            spread = jnp.mean(centred * centred, axis=-1, keepdims=True)
            normed = (
                centred * lax.rsqrt(spread + EPS) * (1.0 + fmod[1:2, :]) + fmod[0:1, :]
            ).astype(BF16)
            velocity = jnp.dot(normed, WF[...], preferred_element_type=F32)
            ZS[:, 0:latents] = (Z[t, pos][:, :latents].astype(F32) + velocity).astype(BF16)
            for i in range(GROUP):
                remote(ZS, Z.at[t + 1, pos], send_sem.at[4], z_sem.at[t + 1], i).start()
            wait_for(Z.at[t], send_sem.at[4])

        wait_for(SB, send_sem.at[1])
        wait_for(CR.at[par], send_sem.at[2])
        return carry

    lax.fori_loop(0, ticks, tick, 0)

    @pl.when(first)
    def _():
        wait_for(Z.at[ticks], z_sem.at[ticks])
        z = Z[ticks, pos][:, :latents]
        for c in range(CHUNKS):
            hout[:, cols[c]] = embed(z, c)

    @pl.when(jnp.logical_not(first))
    def _():
        wait_for(Z.at[ticks, pos], z_sem.at[ticks])
        for c in range(CHUNKS):
            wait_for(X.at[ticks, pos, :, cols[c]], relay_sem.at[ticks, c])
        hout[...] = X[ticks, pos]

    lout[...] = Z[ticks, pos][:, :latents]


def body(
    sections, hidden_in, latent_in, w_qkv, w_out, stale_kv, qk_gain, block_mod, final_mod,
    w_final, w_embed, patch_flow,
):
    rows, depth = hidden_in.shape
    latents = latent_in.shape[1]
    width = w_qkv.shape[2]
    ticks = patch_flow.shape[0]
    anywhere = pl.BlockSpec(memory_space=pl.ANY)
    vmem = pl.BlockSpec(memory_space=pltpu.VMEM)
    smem = pl.BlockSpec(memory_space=pltpu.SMEM)
    dma = pltpu.SemaphoreType.DMA
    macs = ticks * rows * GROUP * depth * width * 4
    return pl.pallas_call(
        functools.partial(kernel, sections),
        out_shape=(
            jax.ShapeDtypeStruct((rows, depth), BF16),
            jax.ShapeDtypeStruct((rows, latents), BF16),
        ),
        in_specs=[
            anywhere, vmem, anywhere, anywhere, anywhere, vmem, vmem, vmem, anywhere, anywhere,
            smem,
        ],
        out_specs=(vmem, vmem),
        scratch_shapes=[
            pltpu.VMEM((ticks + 1, GROUP, rows, depth), BF16),
            pltpu.VMEM((ticks + 1, GROUP, rows, LANES), BF16),
            pltpu.VMEM((depth, 3 * width), BF16),
            pltpu.VMEM((width, depth), BF16),
            pltpu.VMEM(stale_kv.shape, BF16),
            pltpu.VMEM(w_embed.shape, BF16),
            pltpu.VMEM(w_final.shape, BF16),
            pltpu.VMEM((2, CHIPS, rows, depth), F32),
            pltpu.VMEM((CHIPS, rows, depth), BF16),
            pltpu.VMEM((2, CHIPS, rows, depth), BF16),
            pltpu.VMEM((CHIPS, rows, depth), BF16),
            pltpu.VMEM((2, CHIPS - 1, rows, depth), BF16),
            pltpu.VMEM((rows, depth), F32),
            pltpu.VMEM((rows, depth), BF16),
            pltpu.VMEM((rows, LANES), BF16),
            dma((8,)),
            dma((2, CHUNKS)),
            dma((2, CHUNKS)),
            dma((CHUNKS,)),
            dma,
            dma((ticks + 1, CHUNKS)),
            dma((ticks + 1,)),
            dma((5,)),
        ],
        compiler_params=pltpu.CompilerParams(
            collective_id=0, has_side_effects=True, vmem_limit_bytes=52 * 1024 * 1024
        ),
        cost_estimate=pl.CostEstimate(flops=2 * macs, bytes_accessed=10**7, transcendentals=0),
    )(
        hidden_in, latent_in, w_qkv, w_out, stale_kv, qk_gain, block_mod, final_mod,
        w_final, w_embed, patch_flow,
    )


def solution(mesh):
    in_specs = (
        P(("groups", "section"), None),
        P(("groups", "section"), None),
        P(None, None, "section"),
        P("section", None),
        P("groups", None, "section"),
        P(),
        P("groups", None, None),
        P("groups", None),
        P(),
        P(),
        P(),
    )
    out_specs = (P(("groups", "section"), None), P(("groups", "section"), None))
    sections = mesh.shape["section"] // GROUP
    return jax.shard_map(
        functools.partial(body, sections), mesh=mesh, in_specs=in_specs, out_specs=out_specs,
        check_vma=False,
    )
```

```python
import functools
import math

import jax
import jax.numpy as jnp
from jax import lax
from jax.experimental import pallas as pl
from jax.experimental.pallas import tpu as pltpu
from jax.sharding import PartitionSpec as P

HS = 128
GROUP = 8
CHIPS = GROUP // 2
CHUNKS = 4
EXTRA = 16
EPS = 1e-06
F32 = jnp.float32
BF16 = jnp.bfloat16
MESH = pl.DeviceIdType.MESH


def wait_for(ref, sem):
    pltpu.make_async_copy(ref, ref, sem).wait()


def kernel(
    sections,
    hid, lat, wqkv, wout, kv, gain_in, mod_in, fmod_in, wfin, wemb, flow,
    hout, lout,
    X, Z, W, WO, KV, WE, WF, PF, SB, RB, CB, CR, R, ZS,
    gain, mod, fmod, LAT, EX, SW, MH, WC, QKV,
    load_sem, sib_sem, cross_sem, ag_sem, agsib_sem, relay_sem, z_sem, send_sem,
):
    ticks = flow.shape[1]
    rows, depth = hid.shape
    latents = lat.shape[1]
    lanes = 2 * latents
    width = wqkv.shape[2]
    total = kv.shape[1]
    tokens = rows * GROUP
    heads = width // HS
    step = depth // CHUNKS
    cols = [pl.ds(c * step, step) for c in range(CHUNKS)]

    me = lax.axis_index("section")
    sec = me // GROUP
    pos = me % GROUP
    core = pos % 2
    chip = pos // 2
    base = sec * GROUP
    sibling = base + chip * 2 + 1 - core
    low, high = chip % 2, chip // 2
    others = [chip + 1 - 2 * low, chip + 2 - 4 * high, 3 - chip]
    cross = [base + o * 2 + core for o in others]
    first = sec == 0
    last = sec == sections - 1
    after = (me + GROUP) % (sections * GROUP)
    before = (me + (sections - 1) * GROUP) % (sections * GROUP)
    last_base = (sections - 1) * GROUP

    def remote(src, dst, send, recv, target):
        return pltpu.make_async_remote_copy(
            src_ref=src, dst_ref=dst, send_sem=send, recv_sem=recv,
            device_id={"section": target}, device_id_type=MESH,
        )

    loads = [
        pltpu.make_async_copy(hid, X.at[0, pos], load_sem.at[0]),
        pltpu.make_async_copy(wqkv.at[0], W.at[:, pl.ds(0, width)], load_sem.at[1]),
        pltpu.make_async_copy(wqkv.at[1], W.at[:, pl.ds(width, width)], load_sem.at[2]),
        pltpu.make_async_copy(wqkv.at[2], W.at[:, pl.ds(2 * width, width)], load_sem.at[3]),
        pltpu.make_async_copy(kv, KV, load_sem.at[4]),
        pltpu.make_async_copy(wout, WO, load_sem.at[5]),
        pltpu.make_async_copy(wemb, WE, load_sem.at[6]),
        pltpu.make_async_copy(wfin, WF, load_sem.at[7]),
        pltpu.make_async_copy(gain_in, gain, load_sem.at[8]),
        pltpu.make_async_copy(fmod_in, fmod, load_sem.at[9]),
        pltpu.make_async_copy(mod_in, mod, load_sem.at[10]),
        pltpu.make_async_copy(lat, LAT, load_sem.at[11]),
    ]
    for load in loads:
        load.start()

    barrier = pltpu.get_barrier_semaphore()

    def greet(target):
        pl.semaphore_signal(barrier, inc=1, device_id={"section": target}, device_id_type=MESH)

    greet(sibling)
    for target in cross:
        greet(target)

    @pl.when(first)
    def _():
        for i in range(GROUP):
            greet(last_base + i)

    @pl.when(last)
    def _():
        for i in range(GROUP):
            greet(i)

    if sections > 2:

        @pl.when(jnp.logical_not(last))
        def _():
            greet(after)

        @pl.when(jnp.logical_not(first))
        def _():
            greet(before)

    if sections == 2:
        pl.semaphore_wait(barrier, CHIPS + GROUP)
    else:
        edge = jnp.logical_or(first, last)

        @pl.when(edge)
        def _():
            pl.semaphore_wait(barrier, CHIPS + GROUP + 1)

        @pl.when(jnp.logical_not(edge))
        def _():
            pl.semaphore_wait(barrier, CHIPS + 2)

    def split(v):
        high_part = v.astype(BF16)
        return high_part, (v - high_part.astype(F32)).astype(BF16)

    def param(k, c):
        return mod[k, pl.ds(sec, 1), cols[c]]

    def prepare():
        ZS[...] = jnp.zeros_like(ZS)
        Z[0, pos] = jnp.zeros((rows, lanes), BF16)
        loads[11].wait()
        Z[0, pos, :, 0:latents] = LAT[...]
        loads[10].wait()
        row = lax.broadcasted_iota(jnp.int32, (EXTRA, step), 0)
        for c in range(CHUNKS):
            parts = split(1.0 + param(1, c)) + split(param(0, c))
            block = jnp.zeros((EXTRA, step), F32)
            for k, v in enumerate(parts):
                block = jnp.where(row == k, v.astype(F32), block)
            EX[:, cols[c]] = block.astype(BF16)

    loads[0].wait()

    def embed(z, c):
        return jnp.dot(z, WE[:, cols[c]], preferred_element_type=F32).astype(BF16)

    def gather(t):
        def forward(c):
            wait_for(X.at[t, pl.ds(0, 3), :, cols[c]], ag_sem.at[c])
            for o in others:
                block = X.at[t, o * 2 + core, :, cols[c]]
                remote(block, block, send_sem.at[0], agsib_sem.at[c], sibling).start()

        def multiply(c, state):
            wait_for(X.at[t, pl.ds(0, CHIPS), :, cols[c]], agsib_sem.at[c])
            x = X[t, :, :, cols[c]].reshape(tokens, step).astype(F32)
            if state is None:
                start = jnp.mean(x, axis=-1, keepdims=True)
            else:
                start = state[0]
            d = x - start
            s1 = jnp.sum(d, axis=-1, keepdims=True)
            s2 = jnp.sum(d * d, axis=-1, keepdims=True)
            y = jnp.concatenate([(d * (1.0 + param(1, c))).astype(BF16), EX[:, cols[c]]], axis=0)
            raw = jnp.dot(y, W[cols[c], :], preferred_element_type=F32)
            if state is None:
                return start, s1, s2, raw
            return start, state[1] + s1, state[2] + s2, state[3] + raw

        for c in range(CHUNKS):

            @pl.when(t > 0)
            def _():
                wait_for(X.at[t, pos, :, cols[c]], relay_sem.at[t, c])

            block = X.at[t, pos, :, cols[c]]
            for target in reversed(cross):
                remote(block, block, send_sem.at[0], ag_sem.at[c], target).start()
            remote(block, block, send_sem.at[0], agsib_sem.at[c], sibling).start()
            if c == 0:

                @pl.when(t == 0)
                def _():
                    prepare()

            if c > 0:
                forward(c - 1)
            if c == 1:

                @pl.when(t == 0)
                def _():
                    for load in loads[1:10]:
                        load.wait()

            if c > 1:
                state = multiply(c - 2, state if c > 2 else None)
        state = multiply(CHUNKS - 2, state)
        forward(CHUNKS - 1)
        start, s1, s2, raw = multiply(CHUNKS - 1, state)
        rest = s1 / depth
        inverse = lax.rsqrt(jnp.maximum(s2 / depth - rest * rest, 0.0) + EPS)
        scale_sums = raw[tokens : tokens + 1] + raw[tokens + 1 : tokens + 2]
        shift_sums = raw[tokens + 2 : tokens + 3] + raw[tokens + 3 : tokens + 4]
        SW[0:1, :] = shift_sums
        QKV[...] = inverse * (raw[:tokens] - rest * scale_sums) + shift_sums
        wait_for(X.at[t, pl.ds(0, GROUP - 1)], send_sem.at[0])

    def fold():
        centre = jnp.mean(WE[...].astype(F32), axis=-1, keepdims=True)
        folded = None
        for c in range(CHUNKS):
            w = WE[:, cols[c]].astype(F32) - centre
            WC[0:latents, cols[c]], WC[latents : 2 * latents, cols[c]] = split(w)
            term = jnp.dot(
                (w * (1.0 + param(1, c))).astype(BF16), W[cols[c], :], preferred_element_type=F32
            )
            folded = term if folded is None else folded + term
        MH[0:latents, :], MH[latents : 2 * latents, :] = split(folded)

    def embedded(t):
        z = Z[t].reshape(tokens, lanes)[:, : 2 * latents]
        squares = None
        for c in range(CHUNKS):
            h = jnp.dot(z, WC[:, cols[c]], preferred_element_type=F32)
            term = jnp.sum(h * h, axis=-1, keepdims=True)
            squares = term if squares is None else squares + term
        inverse = lax.rsqrt(squares / depth + EPS)
        QKV[...] = inverse * jnp.dot(z, MH[...], preferred_element_type=F32) + SW[0:1, :]

    def tick(t, carry):
        par = t % 2

        @pl.when(jnp.logical_and(t > 0, first))
        def _():
            wait_for(Z.at[t], z_sem.at[t])
            embedded(t)

        @pl.when(jnp.logical_and(t > 0, jnp.logical_not(first)))
        def _():
            wait_for(Z.at[t, pos], z_sem.at[t])

        @pl.when(jnp.logical_or(t == 0, jnp.logical_not(first)))
        def _():
            gather(t)

        qkv = QKV[...]

        def head_norm(v, g):
            return (
                v * lax.rsqrt(jnp.mean(v * v, axis=-1, keepdims=True) + EPS) * g
            ).astype(BF16)

        patch = flow[sec, t]
        outs = []
        for h in range(heads):
            at = slice(h * HS, (h + 1) * HS)
            qn = head_norm(qkv[:, at], gain[sec, 0:1, :])
            kn = head_norm(qkv[:, width + h * HS : width + (h + 1) * HS], gain[sec, 1:2, :])
            vb = qkv[:, 2 * width + h * HS : 2 * width + (h + 1) * HS].astype(BF16)
            for which, fresh in ((0, kn), (1, vb)):
                for j in range(total // tokens):
                    place = slice(j * tokens, (j + 1) * tokens)
                    KV[which, place, at] = jnp.where(
                        patch == j, fresh.astype(F32), KV[which, place, at].astype(F32)
                    ).astype(BF16)
            scores = lax.dot_general(
                qn, KV[0, :, at], (((1,), (1,)), ((), ())), preferred_element_type=F32
            ) * (1.0 / math.sqrt(HS))
            e = jnp.exp(scores)
            totals = jnp.sum(e, axis=-1, keepdims=True)
            mixed = jnp.dot(e.astype(BF16), KV[1, :, at], preferred_element_type=F32)
            outs.append((mixed / totals).astype(BF16))
        attended = jnp.concatenate(outs, axis=1)

        def project(c):
            product = jnp.dot(attended, WO[:, cols[c]], preferred_element_type=F32)
            product = product.reshape(CHIPS, 2, rows, step)
            for side in range(2):
                PF[side, :, :, cols[c]] = product[:, side]
            SB[:, :, cols[c]] = PF[1 - core, :, :, cols[c]].astype(BF16)
            remote(
                SB.at[:, :, cols[c]], RB.at[par, :, :, cols[c]],
                send_sem.at[1], sib_sem.at[par, c], sibling,
            ).start()

        def share(c):
            wait_for(RB.at[par, :, :, cols[c]], sib_sem.at[par, c])
            both = PF[core, :, :, cols[c]] + RB[par, :, :, cols[c]].astype(F32)
            PF[core, :, :, cols[c]] = both
            CB[:, :, cols[c]] = both.astype(BF16)
            for r in reversed(range(CHIPS - 1)):
                remote(
                    CB.at[others[r], :, cols[c]], CR.at[par, r, :, cols[c]],
                    send_sem.at[2], cross_sem.at[par, c], cross[r],
                ).start()

        for c in range(CHUNKS):
            project(c)
            if c > 0:
                share(c - 1)
        share(CHUNKS - 1)

        @pl.when(jnp.logical_and(t > 0, first))
        def _():
            z = Z[t, pos][:, :latents]
            for c in range(CHUNKS):
                X[t, pos, :, cols[c]] = embed(z, c)

        for c in range(CHUNKS):
            wait_for(CR.at[par, :, :, cols[c]], cross_sem.at[par, c])
            summed = PF[core, chip, :, cols[c]]
            for r in range(CHIPS - 1):
                summed = summed + CR[par, r, :, cols[c]].astype(F32)
            result = X[t, pos, :, cols[c]].astype(F32) + param(2, c) * summed
            R[:, cols[c]] = result.astype(BF16)

            @pl.when(jnp.logical_not(last))
            def _():
                remote(
                    R.at[:, cols[c]], X.at[t + 1, pos, :, cols[c]],
                    send_sem.at[3], relay_sem.at[t + 1, c], after,
                ).start()

        @pl.when(jnp.logical_not(last))
        def _():
            copy = remote(Z.at[t, pos], Z.at[t + 1, pos], send_sem.at[4], z_sem.at[t + 1], after)
            copy.start()
            wait_for(Z.at[t, pos], send_sem.at[4])
            wait_for(R, send_sem.at[3])

        @pl.when(last)
        def _():
            x = R[...].astype(F32)
            centred = x - jnp.mean(x, axis=-1, keepdims=True)
            spread = jnp.mean(centred * centred, axis=-1, keepdims=True)
            normed = (
                centred * lax.rsqrt(spread + EPS) * (1.0 + fmod[1:2, :]) + fmod[0:1, :]
            ).astype(BF16)
            velocity = lax.dot_general(
                normed, WF[...], (((1,), (1,)), ((), ())), preferred_element_type=F32
            )
            renewed = (Z[t, pos][:, :latents].astype(F32) + velocity).astype(BF16)
            ZS[...] = jnp.concatenate([renewed, renewed], axis=1)
            for i in range(GROUP):
                remote(ZS, Z.at[t + 1, pos], send_sem.at[4], z_sem.at[t + 1], i).start()
            wait_for(Z.at[t], send_sem.at[4])

        @pl.when(jnp.logical_and(t == 0, first))
        def _():
            fold()

        wait_for(SB, send_sem.at[1])
        wait_for(CR.at[par], send_sem.at[2])
        return carry

    lax.fori_loop(0, ticks, tick, 0)

    @pl.when(first)
    def _():
        wait_for(Z.at[ticks], z_sem.at[ticks])
        z = Z[ticks, pos][:, :latents]
        for c in range(CHUNKS):
            hout[:, cols[c]] = embed(z, c)

    @pl.when(jnp.logical_not(first))
    def _():
        wait_for(Z.at[ticks, pos], z_sem.at[ticks])
        for c in range(CHUNKS):
            wait_for(X.at[ticks, pos, :, cols[c]], relay_sem.at[ticks, c])
        hout[...] = X[ticks, pos]

    lout[...] = Z[ticks, pos][:, :latents]


def body(
    sections, hidden_in, latent_in, w_qkv, w_out, stale_kv, qk_gain, block_mod, final_mod,
    w_final, w_embed, patch_flow,
):
    rows, depth = hidden_in.shape
    latents = latent_in.shape[1]
    lanes = 2 * latents
    width = w_qkv.shape[2]
    ticks = patch_flow.shape[0]
    anywhere = pl.BlockSpec(memory_space=pltpu.HBM)
    vmem = pl.BlockSpec(memory_space=pltpu.VMEM)
    smem = pl.BlockSpec(memory_space=pltpu.SMEM)
    dma = pltpu.SemaphoreType.DMA
    macs = ticks * rows * GROUP * depth * width * 4
    return pl.pallas_call(
        functools.partial(kernel, sections),
        out_shape=(
            jax.ShapeDtypeStruct((rows, depth), BF16),
            jax.ShapeDtypeStruct((rows, latents), BF16),
        ),
        in_specs=[
            anywhere, anywhere, anywhere, anywhere, anywhere, anywhere, anywhere, anywhere,
            anywhere, anywhere, smem,
        ],
        out_specs=(vmem, vmem),
        scratch_shapes=[
            pltpu.VMEM((ticks + 1, GROUP, rows, depth), BF16),
            pltpu.VMEM((ticks + 1, GROUP, rows, lanes), BF16),
            pltpu.VMEM((depth, 3 * width), BF16),
            pltpu.VMEM((width, depth), BF16),
            pltpu.VMEM(stale_kv.shape, BF16),
            pltpu.VMEM(w_embed.shape, BF16),
            pltpu.VMEM((latents, depth), BF16),
            pltpu.VMEM((2, CHIPS, rows, depth), F32),
            pltpu.VMEM((CHIPS, rows, depth), BF16),
            pltpu.VMEM((2, CHIPS, rows, depth), BF16),
            pltpu.VMEM((CHIPS, rows, depth), BF16),
            pltpu.VMEM((2, CHIPS - 1, rows, depth), BF16),
            pltpu.VMEM((rows, depth), BF16),
            pltpu.VMEM((rows, lanes), BF16),
            pltpu.VMEM(qk_gain.shape, F32),
            pltpu.VMEM((3, sections, depth), F32),
            pltpu.VMEM(final_mod.shape, F32),
            pltpu.VMEM((rows, latents), BF16),
            pltpu.VMEM((EXTRA, depth), BF16),
            pltpu.VMEM((8, 3 * width), F32),
            pltpu.VMEM((lanes, 3 * width), BF16),
            pltpu.VMEM((lanes, depth), BF16),
            pltpu.VMEM((rows * GROUP, 3 * width), F32),
            dma((12,)),
            dma((2, CHUNKS)),
            dma((2, CHUNKS)),
            dma((CHUNKS,)),
            dma((CHUNKS,)),
            dma((ticks + 1, CHUNKS)),
            dma((ticks + 1,)),
            dma((5,)),
        ],
        compiler_params=pltpu.CompilerParams(
            collective_id=0, has_side_effects=True, vmem_limit_bytes=64 * 1024 * 1024
        ),
        cost_estimate=pl.CostEstimate(flops=2 * macs, bytes_accessed=10**7, transcendentals=0),
    )(
        hidden_in, latent_in, w_qkv, w_out, stale_kv, qk_gain,
        jnp.transpose(block_mod, (1, 0, 2)), final_mod, w_final.T, w_embed, patch_flow.T,
    )


def solution(mesh):
    in_specs = (
        P(("groups", "section"), None),
        P(("groups", "section"), None),
        P(None, None, "section"),
        P("section", None),
        P("groups", None, "section"),
        P(),
        P("groups", None, None),
        P("groups", None),
        P(),
        P(),
        P(),
    )
    out_specs = (P(("groups", "section"), None), P(("groups", "section"), None))
    sections = mesh.shape["section"] // GROUP
    return jax.shard_map(
        functools.partial(body, sections), mesh=mesh, in_specs=in_specs, out_specs=out_specs,
        check_vma=False,
    )
```

```python
import functools
import math

import jax
import jax.numpy as jnp
from jax import lax
from jax.experimental import pallas as pl
from jax.experimental.pallas import tpu as pltpu
from jax.sharding import PartitionSpec as P

HS = 128
GROUP = 8
CHIPS = GROUP // 2
CHUNKS = 3
EXTRA = 16
LAG = 2
EPS = 1e-06
F32 = jnp.float32
BF16 = jnp.bfloat16
MESH = pl.DeviceIdType.MESH


def wait_for(ref, sem):
    pltpu.make_async_copy(ref, ref, sem).wait()


def kernel(
    sections,
    hid, lat, wqkv, wout, kv, gain_in, mod_in, fmod_in, wfin, wemb, flow,
    hout, lout,
    X, Z, W, WO, KV, WE, WF, PF, SB, RB, CB, CR, R, ZS,
    gain, mod, fmod, LAT, EX, SW, MH, WC, QKV,
    load_sem, sib_sem, cross_sem, ag_sem, agsib_sem, relay_sem, z_sem, send_sem,
):
    ticks = flow.shape[1]
    rows, depth = hid.shape
    latents = lat.shape[1]
    lanes = 2 * latents
    width = wqkv.shape[2]
    total = kv.shape[1]
    tokens = rows * GROUP
    heads = width // HS
    step = depth // CHUNKS
    cols = [pl.ds(c * step, step) for c in range(CHUNKS)]

    me = lax.axis_index("section")
    sec = me // GROUP
    pos = me % GROUP
    core = pos % 2
    chip = pos // 2
    base = sec * GROUP
    sibling = base + chip * 2 + 1 - core
    low, high = chip % 2, chip // 2
    others = [chip + 1 - 2 * low, chip + 2 - 4 * high, 3 - chip]
    order = [2, core, 1 - core]

    def other(r):
        if isinstance(r, int):
            return others[r]
        return chip + (1 - r) * (1 - 2 * low) + r * (2 - 4 * high)

    def peer(r):
        return base + other(r) * 2 + core

    first = sec == 0
    last = sec == sections - 1
    after = (me + GROUP) % (sections * GROUP)
    before = (me + (sections - 1) * GROUP) % (sections * GROUP)
    last_base = (sections - 1) * GROUP

    def remote(src, dst, send, recv, target):
        return pltpu.make_async_remote_copy(
            src_ref=src, dst_ref=dst, send_sem=send, recv_sem=recv,
            device_id={"section": target}, device_id_type=MESH,
        )

    loads = [
        pltpu.make_async_copy(hid, X.at[0, chip, core], load_sem.at[0]),
        pltpu.make_async_copy(wqkv.at[0], W.at[:, pl.ds(0, width)], load_sem.at[1]),
        pltpu.make_async_copy(wqkv.at[1], W.at[:, pl.ds(width, width)], load_sem.at[2]),
        pltpu.make_async_copy(wqkv.at[2], W.at[:, pl.ds(2 * width, width)], load_sem.at[3]),
        pltpu.make_async_copy(kv, KV, load_sem.at[4]),
        pltpu.make_async_copy(wout, WO, load_sem.at[5]),
        pltpu.make_async_copy(wemb, WE, load_sem.at[6]),
        pltpu.make_async_copy(wfin, WF, load_sem.at[7]),
        pltpu.make_async_copy(gain_in, gain, load_sem.at[8]),
        pltpu.make_async_copy(fmod_in, fmod, load_sem.at[9]),
        pltpu.make_async_copy(mod_in, mod, load_sem.at[10]),
        pltpu.make_async_copy(lat, LAT, load_sem.at[11]),
    ]
    for load in loads:
        load.start()

    barrier = pltpu.get_barrier_semaphore()

    def greet(target):
        pl.semaphore_signal(barrier, inc=1, device_id={"section": target}, device_id_type=MESH)

    greet(sibling)
    for r in range(CHIPS - 1):
        greet(peer(r))

    @pl.when(first)
    def _():
        for i in range(GROUP):
            greet(last_base + i)

    @pl.when(last)
    def _():
        for i in range(GROUP):
            greet(i)

    if sections > 2:

        @pl.when(jnp.logical_not(last))
        def _():
            greet(after)

        @pl.when(jnp.logical_not(first))
        def _():
            greet(before)

    if sections == 2:
        pl.semaphore_wait(barrier, CHIPS + GROUP)
    else:
        edge = jnp.logical_or(first, last)

        @pl.when(edge)
        def _():
            pl.semaphore_wait(barrier, CHIPS + GROUP + 1)

        @pl.when(jnp.logical_not(edge))
        def _():
            pl.semaphore_wait(barrier, CHIPS + 2)

    def split(v):
        high_part = v.astype(BF16)
        return high_part, (v - high_part.astype(F32)).astype(BF16)

    def param(k, c):
        return mod[k, pl.ds(sec, 1), cols[c]]

    def prepare():
        ZS[...] = jnp.zeros_like(ZS)
        Z[0, pos] = jnp.zeros((rows, lanes), BF16)
        loads[11].wait()
        Z[0, pos, :, 0:latents] = LAT[...]
        loads[10].wait()
        row = lax.broadcasted_iota(jnp.int32, (EXTRA, step), 0)
        for c in range(CHUNKS):
            parts = split(1.0 + param(1, c)) + split(param(0, c))
            block = jnp.zeros((EXTRA, step), F32)
            for k, v in enumerate(parts):
                block = jnp.where(row == k, v.astype(F32), block)
            EX[:, cols[c]] = block.astype(BF16)

    loads[0].wait()

    def embed(z, c):
        return jnp.dot(z, WE[:, cols[c]], preferred_element_type=F32).astype(BF16)

    def gather(t):
        def forward(c):
            wait_for(X.at[t, pl.ds(0, CHIPS - 1), 0, :, cols[c]], ag_sem.at[c])
            blocks = X.at[t, :, core, :, cols[c]]
            remote(blocks, blocks, send_sem.at[5], agsib_sem.at[c], sibling).start()

        def multiply(c, state):
            wait_for(X.at[t, :, 0, :, cols[c]], agsib_sem.at[c])
            x = X[t, :, :, :, cols[c]].reshape(tokens, step).astype(F32)
            if state is None:
                start = jnp.mean(x, axis=-1, keepdims=True)
            else:
                start = state[0]
            d = x - start
            s1 = jnp.sum(d, axis=-1, keepdims=True)
            s2 = jnp.sum(d * d, axis=-1, keepdims=True)
            y = jnp.concatenate([(d * (1.0 + param(1, c))).astype(BF16), EX[:, cols[c]]], axis=0)
            raw = jnp.dot(y, W[cols[c], :], preferred_element_type=F32)
            if state is None:
                return start, s1, s2, raw
            return start, state[1] + s1, state[2] + s2, state[3] + raw

        state = None
        for c in range(CHUNKS):

            @pl.when(t > 0)
            def _():
                wait_for(X.at[t, chip, core, :, cols[c]], relay_sem.at[t, c])

            block = X.at[t, chip, core, :, cols[c]]
            for r in order:
                remote(block, block, send_sem.at[0], ag_sem.at[c], peer(r)).start()
            if c == 0:

                @pl.when(t == 0)
                def _():
                    prepare()

            if c > 0:
                forward(c - 1)
            if c == 1:

                @pl.when(t == 0)
                def _():
                    for load in loads[1:10]:
                        load.wait()

            if c > 1:
                state = multiply(c - 2, state)
        state = multiply(CHUNKS - 2, state)
        forward(CHUNKS - 1)
        start, s1, s2, raw = multiply(CHUNKS - 1, state)
        rest = s1 / depth
        inverse = lax.rsqrt(jnp.maximum(s2 / depth - rest * rest, 0.0) + EPS)
        scale_sums = raw[tokens : tokens + 1] + raw[tokens + 1 : tokens + 2]
        shift_sums = raw[tokens + 2 : tokens + 3] + raw[tokens + 3 : tokens + 4]
        SW[0:1, :] = shift_sums
        QKV[...] = inverse * (raw[:tokens] - rest * scale_sums) + shift_sums
        wait_for(X.at[t, pl.ds(0, CHIPS - 1), 0], send_sem.at[0])
        wait_for(X.at[t, :, 0], send_sem.at[5])

    def fold():
        centre = jnp.mean(WE[...].astype(F32), axis=-1, keepdims=True)
        folded = None
        for c in range(CHUNKS):
            w = WE[:, cols[c]].astype(F32) - centre
            WC[0:latents, cols[c]], WC[latents : 2 * latents, cols[c]] = split(w)
            term = jnp.dot(
                (w * (1.0 + param(1, c))).astype(BF16), W[cols[c], :], preferred_element_type=F32
            )
            folded = term if folded is None else folded + term
        MH[0:latents, :], MH[latents : 2 * latents, :] = split(folded)

    def embedded(t):
        z = Z[t].reshape(tokens, lanes)[:, : 2 * latents]
        squares = None
        for c in range(CHUNKS):
            h = jnp.dot(z, WC[:, cols[c]], preferred_element_type=F32)
            term = jnp.sum(h * h, axis=-1, keepdims=True)
            squares = term if squares is None else squares + term
        inverse = lax.rsqrt(squares / depth + EPS)
        QKV[...] = inverse * jnp.dot(z, MH[...], preferred_element_type=F32) + SW[0:1, :]

    def tick(t, carry):
        par = t % 2

        @pl.when(jnp.logical_and(t > 0, first))
        def _():
            wait_for(Z.at[t], z_sem.at[t])
            embedded(t)

        @pl.when(jnp.logical_and(t > 0, jnp.logical_not(first)))
        def _():
            wait_for(Z.at[t, pos], z_sem.at[t])

        @pl.when(jnp.logical_or(t == 0, jnp.logical_not(first)))
        def _():
            gather(t)

        qkv = QKV[...]

        def head_norm(v, g):
            return (
                v * lax.rsqrt(jnp.mean(v * v, axis=-1, keepdims=True) + EPS) * g
            ).astype(BF16)

        patch = flow[sec, t]
        outs = []
        for h in range(heads):
            at = slice(h * HS, (h + 1) * HS)
            qn = head_norm(qkv[:, at], gain[sec, 0:1, :])
            kn = head_norm(qkv[:, width + h * HS : width + (h + 1) * HS], gain[sec, 1:2, :])
            vb = qkv[:, 2 * width + h * HS : 2 * width + (h + 1) * HS].astype(BF16)
            for which, fresh in ((0, kn), (1, vb)):
                for j in range(total // tokens):
                    place = slice(j * tokens, (j + 1) * tokens)
                    KV[which, place, at] = jnp.where(
                        patch == j, fresh.astype(F32), KV[which, place, at].astype(F32)
                    ).astype(BF16)
            scores = lax.dot_general(
                qn, KV[0, :, at], (((1,), (1,)), ((), ())), preferred_element_type=F32
            ) * (1.0 / math.sqrt(HS))
            e = jnp.exp(scores)
            totals = jnp.sum(e, axis=-1, keepdims=True)
            mixed = jnp.dot(e.astype(BF16), KV[1, :, at], preferred_element_type=F32)
            outs.append((mixed / totals).astype(BF16))
        attended = jnp.concatenate(outs, axis=1)

        def project(c):
            product = jnp.dot(attended, WO[:, cols[c]], preferred_element_type=F32)
            product = product.reshape(CHIPS, 2, rows, step)
            for side in range(2):
                PF[side, :, :, cols[c]] = product[:, side]
            SB[:, :, cols[c]] = PF[1 - core, :, :, cols[c]].astype(BF16)
            remote(
                SB.at[:, :, cols[c]], RB.at[par, :, :, cols[c]],
                send_sem.at[1], sib_sem.at[par, c], sibling,
            ).start()

        def share(c):
            wait_for(RB.at[par, :, :, cols[c]], sib_sem.at[par, c])
            both = PF[core, :, :, cols[c]] + RB[par, :, :, cols[c]].astype(F32)
            PF[core, :, :, cols[c]] = both
            CB[:, :, cols[c]] = both.astype(BF16)
            for r in order:
                remote(
                    CB.at[other(r), :, cols[c]], CR.at[par, r, :, cols[c]],
                    send_sem.at[2], cross_sem.at[par, c], peer(r),
                ).start()

        for c in range(CHUNKS):
            project(c)
            if c >= LAG:
                share(c - LAG)
        for c in range(CHUNKS - LAG, CHUNKS):
            share(c)

        @pl.when(jnp.logical_and(t > 0, first))
        def _():
            z = Z[t, pos][:, :latents]
            for c in range(CHUNKS):
                X[t, chip, core, :, cols[c]] = embed(z, c)

        for c in range(CHUNKS):
            wait_for(CR.at[par, :, :, cols[c]], cross_sem.at[par, c])
            summed = PF[core, chip, :, cols[c]]
            for r in range(CHIPS - 1):
                summed = summed + CR[par, r, :, cols[c]].astype(F32)
            result = X[t, chip, core, :, cols[c]].astype(F32) + param(2, c) * summed
            R[:, cols[c]] = result.astype(BF16)

            @pl.when(jnp.logical_not(last))
            def _():
                remote(
                    R.at[:, cols[c]], X.at[t + 1, chip, core, :, cols[c]],
                    send_sem.at[3], relay_sem.at[t + 1, c], after,
                ).start()

        @pl.when(jnp.logical_not(last))
        def _():
            copy = remote(Z.at[t, pos], Z.at[t + 1, pos], send_sem.at[4], z_sem.at[t + 1], after)
            copy.start()
            wait_for(Z.at[t, pos], send_sem.at[4])
            wait_for(R, send_sem.at[3])

        @pl.when(last)
        def _():
            x = R[...].astype(F32)
            centred = x - jnp.mean(x, axis=-1, keepdims=True)
            spread = jnp.mean(centred * centred, axis=-1, keepdims=True)
            normed = (
                centred * lax.rsqrt(spread + EPS) * (1.0 + fmod[1:2, :]) + fmod[0:1, :]
            ).astype(BF16)
            velocity = lax.dot_general(
                normed, WF[...], (((1,), (1,)), ((), ())), preferred_element_type=F32
            )
            renewed = (Z[t, pos][:, :latents].astype(F32) + velocity).astype(BF16)
            ZS[...] = jnp.concatenate([renewed, renewed], axis=1)
            for i in range(GROUP):
                remote(ZS, Z.at[t + 1, pos], send_sem.at[4], z_sem.at[t + 1], i).start()
            wait_for(Z.at[t], send_sem.at[4])

        @pl.when(jnp.logical_and(t == 0, first))
        def _():
            fold()

        wait_for(SB, send_sem.at[1])
        wait_for(CR.at[par], send_sem.at[2])
        return carry

    lax.fori_loop(0, ticks, tick, 0)

    @pl.when(first)
    def _():
        wait_for(Z.at[ticks], z_sem.at[ticks])
        z = Z[ticks, pos][:, :latents]
        for c in range(CHUNKS):
            hout[:, cols[c]] = embed(z, c)

    @pl.when(jnp.logical_not(first))
    def _():
        wait_for(Z.at[ticks, pos], z_sem.at[ticks])
        for c in range(CHUNKS):
            wait_for(X.at[ticks, chip, core, :, cols[c]], relay_sem.at[ticks, c])
        hout[...] = X[ticks, chip, core]

    lout[...] = Z[ticks, pos][:, :latents]


def body(
    sections, hidden_in, latent_in, w_qkv, w_out, stale_kv, qk_gain, block_mod, final_mod,
    w_final, w_embed, patch_flow,
):
    rows, depth = hidden_in.shape
    latents = latent_in.shape[1]
    lanes = 2 * latents
    width = w_qkv.shape[2]
    ticks = patch_flow.shape[0]
    anywhere = pl.BlockSpec(memory_space=pltpu.HBM)
    vmem = pl.BlockSpec(memory_space=pltpu.VMEM)
    smem = pl.BlockSpec(memory_space=pltpu.SMEM)
    dma = pltpu.SemaphoreType.DMA
    macs = ticks * rows * GROUP * depth * width * 4
    return pl.pallas_call(
        functools.partial(kernel, sections),
        out_shape=(
            jax.ShapeDtypeStruct((rows, depth), BF16),
            jax.ShapeDtypeStruct((rows, latents), BF16),
        ),
        in_specs=[
            anywhere, anywhere, anywhere, anywhere, anywhere, anywhere, anywhere, anywhere,
            anywhere, anywhere, smem,
        ],
        out_specs=(vmem, vmem),
        scratch_shapes=[
            pltpu.VMEM((ticks + 1, CHIPS, 2, rows, depth), BF16),
            pltpu.VMEM((ticks + 1, GROUP, rows, lanes), BF16),
            pltpu.VMEM((depth, 3 * width), BF16),
            pltpu.VMEM((width, depth), BF16),
            pltpu.VMEM(stale_kv.shape, BF16),
            pltpu.VMEM(w_embed.shape, BF16),
            pltpu.VMEM((latents, depth), BF16),
            pltpu.VMEM((2, CHIPS, rows, depth), F32),
            pltpu.VMEM((CHIPS, rows, depth), BF16),
            pltpu.VMEM((2, CHIPS, rows, depth), BF16),
            pltpu.VMEM((CHIPS, rows, depth), BF16),
            pltpu.VMEM((2, CHIPS - 1, rows, depth), BF16),
            pltpu.VMEM((rows, depth), BF16),
            pltpu.VMEM((rows, lanes), BF16),
            pltpu.VMEM(qk_gain.shape, F32),
            pltpu.VMEM((3, sections, depth), F32),
            pltpu.VMEM(final_mod.shape, F32),
            pltpu.VMEM((rows, latents), BF16),
            pltpu.VMEM((EXTRA, depth), BF16),
            pltpu.VMEM((8, 3 * width), F32),
            pltpu.VMEM((lanes, 3 * width), BF16),
            pltpu.VMEM((lanes, depth), BF16),
            pltpu.VMEM((rows * GROUP, 3 * width), F32),
            dma((12,)),
            dma((2, CHUNKS)),
            dma((2, CHUNKS)),
            dma((CHUNKS,)),
            dma((CHUNKS,)),
            dma((ticks + 1, CHUNKS)),
            dma((ticks + 1,)),
            dma((6,)),
        ],
        compiler_params=pltpu.CompilerParams(
            collective_id=0, has_side_effects=True, vmem_limit_bytes=64 * 1024 * 1024
        ),
        cost_estimate=pl.CostEstimate(flops=2 * macs, bytes_accessed=10**7, transcendentals=0),
    )(
        hidden_in, latent_in, w_qkv, w_out, stale_kv, qk_gain,
        jnp.transpose(block_mod, (1, 0, 2)), final_mod, w_final.T, w_embed, patch_flow.T,
    )


def solution(mesh):
    in_specs = (
        P(("groups", "section"), None),
        P(("groups", "section"), None),
        P(None, None, "section"),
        P("section", None),
        P("groups", None, "section"),
        P(),
        P("groups", None, None),
        P("groups", None),
        P(),
        P(),
        P(),
    )
    out_specs = (P(("groups", "section"), None), P(("groups", "section"), None))
    sections = mesh.shape["section"] // GROUP
    return jax.shard_map(
        functools.partial(body, sections), mesh=mesh, in_specs=in_specs, out_specs=out_specs,
        check_vma=False,
    )
```

```python
import functools
import math

import jax
import jax.numpy as jnp
from jax import lax
from jax.experimental import pallas as pl
from jax.experimental.pallas import tpu as pltpu
from jax.sharding import PartitionSpec as P

HS = 128
GROUP = 8
CHIPS = GROUP // 2
SHARES = (5, 4, 3)
CHUNKS = len(SHARES)
EXTRA = 16
LAG = 2
EPS = 1e-06
F32 = jnp.float32
BF16 = jnp.bfloat16
MESH = pl.DeviceIdType.MESH


def wait_for(ref, sem):
    pltpu.make_async_copy(ref, ref, sem).wait()


def kernel(
    sections,
    hid, lat, wqkv, wout, kv, gain_in, mod_in, fmod_in, wfin, wemb, flow,
    hout, lout,
    X, Z, W, WO, KV, WE, WF, PF, SB, RB, CB, CR, R, ZS,
    gain, mod, fmod, LAT, EX, SW, MH, WC, QKV,
    load_sem, sib_sem, cross_sem, ag_sem, agsib_sem, relay_sem, z_sem, send_sem,
):
    ticks = flow.shape[1]
    rows, depth = hid.shape
    latents = lat.shape[1]
    lanes = 2 * latents
    width = wqkv.shape[2]
    total = kv.shape[1]
    tokens = rows * GROUP
    heads = width // HS
    unit = depth // sum(SHARES)
    steps = [share * unit for share in SHARES]
    cols = [pl.ds(sum(steps[:c]), steps[c]) for c in range(CHUNKS)]

    me = lax.axis_index("section")
    sec = me // GROUP
    pos = me % GROUP
    core = pos % 2
    chip = pos // 2
    base = sec * GROUP
    sibling = base + chip * 2 + 1 - core
    low, high = chip % 2, chip // 2
    others = [chip + 1 - 2 * low, chip + 2 - 4 * high, 3 - chip]
    order = [2, core, 1 - core]

    def other(r):
        if isinstance(r, int):
            return others[r]
        return chip + (1 - r) * (1 - 2 * low) + r * (2 - 4 * high)

    def peer(r):
        return base + other(r) * 2 + core

    first = sec == 0
    last = sec == sections - 1
    after = (me + GROUP) % (sections * GROUP)
    before = (me + (sections - 1) * GROUP) % (sections * GROUP)
    last_base = (sections - 1) * GROUP

    def remote(src, dst, send, recv, target):
        return pltpu.make_async_remote_copy(
            src_ref=src, dst_ref=dst, send_sem=send, recv_sem=recv,
            device_id={"section": target}, device_id_type=MESH,
        )

    loads = [
        pltpu.make_async_copy(hid, X.at[0, chip, core], load_sem.at[0]),
        pltpu.make_async_copy(wqkv.at[0], W.at[:, pl.ds(0, width)], load_sem.at[1]),
        pltpu.make_async_copy(wqkv.at[1], W.at[:, pl.ds(width, width)], load_sem.at[2]),
        pltpu.make_async_copy(wqkv.at[2], W.at[:, pl.ds(2 * width, width)], load_sem.at[3]),
        pltpu.make_async_copy(kv, KV, load_sem.at[4]),
        pltpu.make_async_copy(wout, WO, load_sem.at[5]),
        pltpu.make_async_copy(wemb, WE, load_sem.at[6]),
        pltpu.make_async_copy(wfin, WF, load_sem.at[7]),
        pltpu.make_async_copy(gain_in, gain, load_sem.at[8]),
        pltpu.make_async_copy(fmod_in, fmod, load_sem.at[9]),
        pltpu.make_async_copy(mod_in, mod, load_sem.at[10]),
        pltpu.make_async_copy(lat, LAT, load_sem.at[11]),
    ]
    for load in loads:
        load.start()

    barrier = pltpu.get_barrier_semaphore()

    def greet(target):
        pl.semaphore_signal(barrier, inc=1, device_id={"section": target}, device_id_type=MESH)

    greet(sibling)
    for r in range(CHIPS - 1):
        greet(peer(r))

    @pl.when(first)
    def _():
        for i in range(GROUP):
            greet(last_base + i)

    @pl.when(last)
    def _():
        for i in range(GROUP):
            greet(i)

    if sections > 2:

        @pl.when(jnp.logical_not(last))
        def _():
            greet(after)

        @pl.when(jnp.logical_not(first))
        def _():
            greet(before)

    if sections == 2:
        pl.semaphore_wait(barrier, CHIPS + GROUP)
    else:
        edge = jnp.logical_or(first, last)

        @pl.when(edge)
        def _():
            pl.semaphore_wait(barrier, CHIPS + GROUP + 1)

        @pl.when(jnp.logical_not(edge))
        def _():
            pl.semaphore_wait(barrier, CHIPS + 2)

    def split(v):
        high_part = v.astype(BF16)
        return high_part, (v - high_part.astype(F32)).astype(BF16)

    def param(k, c):
        return mod[k, pl.ds(sec, 1), cols[c]]

    def extra_rows(scale, shift):
        row = lax.broadcasted_iota(jnp.int32, (EXTRA, scale.shape[1]), 0)
        block = jnp.zeros((EXTRA, scale.shape[1]), F32)
        for k, v in enumerate(split(scale) + split(shift)):
            block = jnp.where(row == k, v.astype(F32), block)
        return block.astype(BF16)

    def accumulate(x, scale, extra, times, state):
        if state is None:
            start = jnp.mean(x, axis=-1, keepdims=True)
        else:
            start = state[0]
        d = x - start
        s1 = jnp.sum(d, axis=-1, keepdims=True)
        s2 = jnp.sum(d * d, axis=-1, keepdims=True)
        raw = times(jnp.concatenate([(d * scale).astype(BF16), extra], axis=0))
        if state is None:
            return start, s1, s2, raw
        return start, state[1] + s1, state[2] + s2, state[3] + raw

    def finish(state):
        start, s1, s2, raw = state
        count = start.shape[0]
        rest = s1 / depth
        inverse = lax.rsqrt(jnp.maximum(s2 / depth - rest * rest, 0.0) + EPS)
        scale_sums = raw[count : count + 1] + raw[count + 1 : count + 2]
        shift_sums = raw[count + 2 : count + 3] + raw[count + 3 : count + 4]
        return inverse * (raw[:count] - rest * scale_sums) + shift_sums, shift_sums

    def prepare():
        ZS[...] = jnp.zeros_like(ZS)
        Z[0, pos] = jnp.zeros((rows, lanes), BF16)
        loads[11].wait()
        Z[0, pos, :, 0:latents] = LAT[...]
        loads[10].wait()
        for c in range(CHUNKS):
            EX[:, cols[c]] = extra_rows(1.0 + param(1, c), param(0, c))

    loads[0].wait()

    def embed(z, c):
        return jnp.dot(z, WE[:, cols[c]], preferred_element_type=F32).astype(BF16)

    def gather(t):
        def forward(c):
            wait_for(X.at[t, pl.ds(0, CHIPS - 1), 0, :, cols[c]], ag_sem.at[c])
            blocks = X.at[t, :, core, :, cols[c]]
            remote(blocks, blocks, send_sem.at[5], agsib_sem.at[c], sibling).start()

        def multiply(c, state):
            wait_for(X.at[t, :, 0, :, cols[c]], agsib_sem.at[c])
            x = X[t, :, :, :, cols[c]].reshape(tokens, steps[c]).astype(F32)

            def times(y):
                return jnp.dot(y, W[cols[c], :], preferred_element_type=F32)

            return accumulate(x, 1.0 + param(1, c), EX[:, cols[c]], times, state)

        state = None
        for c in range(CHUNKS):

            @pl.when(t > 0)
            def _():
                wait_for(X.at[t, chip, core, :, cols[c]], relay_sem.at[t, c])

            block = X.at[t, chip, core, :, cols[c]]
            for r in order:
                remote(block, block, send_sem.at[0], ag_sem.at[c], peer(r)).start()
            if c == 0:

                @pl.when(t == 0)
                def _():
                    prepare()

            if c > 0:
                forward(c - 1)
            if c == 1:

                @pl.when(t == 0)
                def _():
                    for load in loads[1:10]:
                        load.wait()

            if c > 1:
                state = multiply(c - 2, state)
        state = multiply(CHUNKS - 2, state)
        forward(CHUNKS - 1)
        values, shift_sums = finish(multiply(CHUNKS - 1, state))
        SW[0:1, :] = shift_sums
        QKV[...] = values
        wait_for(X.at[t, pl.ds(0, CHIPS - 1), 0], send_sem.at[0])
        wait_for(X.at[t, :, 0], send_sem.at[5])

    def fold():
        centre = jnp.mean(WE[...].astype(F32), axis=-1, keepdims=True)
        folded = None
        for c in range(CHUNKS):
            w = WE[:, cols[c]].astype(F32) - centre
            WC[0:latents, cols[c]], WC[latents : 2 * latents, cols[c]] = split(w)
            term = jnp.dot(
                (w * (1.0 + param(1, c))).astype(BF16), W[cols[c], :], preferred_element_type=F32
            )
            folded = term if folded is None else folded + term
        MH[0:latents, :], MH[latents : 2 * latents, :] = split(folded)

    def embedded(t):
        z = Z[t].reshape(tokens, lanes)[:, : 2 * latents]
        squares = None
        for c in range(CHUNKS):
            h = jnp.dot(z, WC[:, cols[c]], preferred_element_type=F32)
            term = jnp.sum(h * h, axis=-1, keepdims=True)
            squares = term if squares is None else squares + term
        inverse = lax.rsqrt(squares / depth + EPS)
        QKV[...] = inverse * jnp.dot(z, MH[...], preferred_element_type=F32) + SW[0:1, :]

    def tick(t, carry):
        par = t % 2

        @pl.when(jnp.logical_and(t > 0, first))
        def _():
            wait_for(Z.at[t], z_sem.at[t])
            embedded(t)

        @pl.when(jnp.logical_and(t > 0, jnp.logical_not(first)))
        def _():
            wait_for(Z.at[t, pos], z_sem.at[t])

        @pl.when(jnp.logical_or(t == 0, jnp.logical_not(first)))
        def _():
            gather(t)

        qkv = QKV[...]

        def head_norm(v, g):
            return (
                v * lax.rsqrt(jnp.mean(v * v, axis=-1, keepdims=True) + EPS) * g
            ).astype(BF16)

        patch = flow[sec, t]
        outs = []
        for h in range(heads):
            at = slice(h * HS, (h + 1) * HS)
            qn = head_norm(qkv[:, at], gain[sec, 0:1, :])
            kn = head_norm(qkv[:, width + h * HS : width + (h + 1) * HS], gain[sec, 1:2, :])
            vb = qkv[:, 2 * width + h * HS : 2 * width + (h + 1) * HS].astype(BF16)
            for which, fresh in ((0, kn), (1, vb)):
                for j in range(total // tokens):
                    place = slice(j * tokens, (j + 1) * tokens)
                    KV[which, place, at] = jnp.where(
                        patch == j, fresh.astype(F32), KV[which, place, at].astype(F32)
                    ).astype(BF16)
            scores = lax.dot_general(
                qn, KV[0, :, at], (((1,), (1,)), ((), ())), preferred_element_type=F32
            ) * (1.0 / math.sqrt(HS))
            e = jnp.exp(scores)
            totals = jnp.sum(e, axis=-1, keepdims=True)
            mixed = jnp.dot(e.astype(BF16), KV[1, :, at], preferred_element_type=F32)
            outs.append((mixed / totals).astype(BF16))
        attended = jnp.concatenate(outs, axis=1)

        def project(c):
            product = jnp.dot(attended, WO[:, cols[c]], preferred_element_type=F32)
            product = product.reshape(CHIPS, 2, rows, steps[c])
            for side in range(2):
                PF[side, :, :, cols[c]] = product[:, side]
            SB[:, :, cols[c]] = PF[1 - core, :, :, cols[c]].astype(BF16)
            remote(
                SB.at[:, :, cols[c]], RB.at[par, :, :, cols[c]],
                send_sem.at[1], sib_sem.at[par, c], sibling,
            ).start()

        def share(c):
            wait_for(RB.at[par, :, :, cols[c]], sib_sem.at[par, c])
            both = PF[core, :, :, cols[c]] + RB[par, :, :, cols[c]].astype(F32)
            PF[core, :, :, cols[c]] = both
            CB[:, :, cols[c]] = both.astype(BF16)
            for r in order:
                remote(
                    CB.at[other(r), :, cols[c]], CR.at[par, r, :, cols[c]],
                    send_sem.at[2], cross_sem.at[par, c], peer(r),
                ).start()

        for c in range(CHUNKS):
            project(c)
            if c >= LAG:
                share(c - LAG)
        for c in range(CHUNKS - LAG, CHUNKS):
            share(c)

        @pl.when(jnp.logical_and(t > 0, first))
        def _():
            z = Z[t, pos][:, :latents]
            for c in range(CHUNKS):
                X[t, chip, core, :, cols[c]] = embed(z, c)

        def combine(c):
            wait_for(CR.at[par, :, :, cols[c]], cross_sem.at[par, c])
            summed = PF[core, chip, :, cols[c]]
            for r in range(CHIPS - 1):
                summed = summed + CR[par, r, :, cols[c]].astype(F32)
            result = X[t, chip, core, :, cols[c]].astype(F32) + param(2, c) * summed
            return result.astype(BF16)

        @pl.when(jnp.logical_not(last))
        def _():
            copy = remote(Z.at[t, pos], Z.at[t + 1, pos], send_sem.at[4], z_sem.at[t + 1], after)
            copy.start()
            for c in range(CHUNKS):
                R[:, cols[c]] = combine(c)
                remote(
                    R.at[:, cols[c]], X.at[t + 1, chip, core, :, cols[c]],
                    send_sem.at[3], relay_sem.at[t + 1, c], after,
                ).start()
            wait_for(Z.at[t, pos], send_sem.at[4])
            wait_for(R, send_sem.at[3])

        @pl.when(last)
        def _():
            state = None
            for c in range(CHUNKS):

                def times(y):
                    return lax.dot_general(
                        y, WF[:, cols[c]], (((1,), (1,)), ((), ())), preferred_element_type=F32
                    )

                scale = 1.0 + fmod[1:2, cols[c]]
                extra = extra_rows(scale, fmod[0:1, cols[c]])
                state = accumulate(combine(c).astype(F32), scale, extra, times, state)
            velocity, _ = finish(state)
            renewed = (Z[t, pos][:, :latents].astype(F32) + velocity).astype(BF16)
            ZS[...] = jnp.concatenate([renewed, renewed], axis=1)
            for i in range(GROUP):
                remote(ZS, Z.at[t + 1, pos], send_sem.at[4], z_sem.at[t + 1], i).start()
            wait_for(Z.at[t], send_sem.at[4])

        @pl.when(jnp.logical_and(t == 0, first))
        def _():
            fold()

        wait_for(SB, send_sem.at[1])
        wait_for(CR.at[par], send_sem.at[2])
        return carry

    lax.fori_loop(0, ticks, tick, 0)

    @pl.when(first)
    def _():
        wait_for(Z.at[ticks], z_sem.at[ticks])
        z = Z[ticks, pos][:, :latents]
        for c in range(CHUNKS):
            hout[:, cols[c]] = embed(z, c)

    @pl.when(jnp.logical_not(first))
    def _():
        wait_for(Z.at[ticks, pos], z_sem.at[ticks])
        for c in range(CHUNKS):
            wait_for(X.at[ticks, chip, core, :, cols[c]], relay_sem.at[ticks, c])
        hout[...] = X[ticks, chip, core]

    lout[...] = Z[ticks, pos][:, :latents]


def body(
    sections, hidden_in, latent_in, w_qkv, w_out, stale_kv, qk_gain, block_mod, final_mod,
    w_final, w_embed, patch_flow,
):
    rows, depth = hidden_in.shape
    latents = latent_in.shape[1]
    lanes = 2 * latents
    width = w_qkv.shape[2]
    ticks = patch_flow.shape[0]
    anywhere = pl.BlockSpec(memory_space=pltpu.HBM)
    vmem = pl.BlockSpec(memory_space=pltpu.VMEM)
    smem = pl.BlockSpec(memory_space=pltpu.SMEM)
    dma = pltpu.SemaphoreType.DMA
    macs = ticks * rows * GROUP * depth * width * 4
    return pl.pallas_call(
        functools.partial(kernel, sections),
        out_shape=(
            jax.ShapeDtypeStruct((rows, depth), BF16),
            jax.ShapeDtypeStruct((rows, latents), BF16),
        ),
        in_specs=[
            anywhere, anywhere, anywhere, anywhere, anywhere, anywhere, anywhere, anywhere,
            anywhere, anywhere, smem,
        ],
        out_specs=(vmem, vmem),
        scratch_shapes=[
            pltpu.VMEM((ticks + 1, CHIPS, 2, rows, depth), BF16),
            pltpu.VMEM((ticks + 1, GROUP, rows, lanes), BF16),
            pltpu.VMEM((depth, 3 * width), BF16),
            pltpu.VMEM((width, depth), BF16),
            pltpu.VMEM(stale_kv.shape, BF16),
            pltpu.VMEM(w_embed.shape, BF16),
            pltpu.VMEM((latents, depth), BF16),
            pltpu.VMEM((2, CHIPS, rows, depth), F32),
            pltpu.VMEM((CHIPS, rows, depth), BF16),
            pltpu.VMEM((2, CHIPS, rows, depth), BF16),
            pltpu.VMEM((CHIPS, rows, depth), BF16),
            pltpu.VMEM((2, CHIPS - 1, rows, depth), BF16),
            pltpu.VMEM((rows, depth), BF16),
            pltpu.VMEM((rows, lanes), BF16),
            pltpu.VMEM(qk_gain.shape, F32),
            pltpu.VMEM((3, sections, depth), F32),
            pltpu.VMEM(final_mod.shape, F32),
            pltpu.VMEM((rows, latents), BF16),
            pltpu.VMEM((EXTRA, depth), BF16),
            pltpu.VMEM((8, 3 * width), F32),
            pltpu.VMEM((lanes, 3 * width), BF16),
            pltpu.VMEM((lanes, depth), BF16),
            pltpu.VMEM((rows * GROUP, 3 * width), F32),
            dma((12,)),
            dma((2, CHUNKS)),
            dma((2, CHUNKS)),
            dma((CHUNKS,)),
            dma((CHUNKS,)),
            dma((ticks + 1, CHUNKS)),
            dma((ticks + 1,)),
            dma((6,)),
        ],
        compiler_params=pltpu.CompilerParams(
            collective_id=0, has_side_effects=True, vmem_limit_bytes=64 * 1024 * 1024
        ),
        cost_estimate=pl.CostEstimate(flops=2 * macs, bytes_accessed=10**7, transcendentals=0),
    )(
        hidden_in, latent_in, w_qkv, w_out, stale_kv, qk_gain,
        jnp.transpose(block_mod, (1, 0, 2)), final_mod, w_final.T, w_embed, patch_flow.T,
    )


def solution(mesh):
    in_specs = (
        P(("groups", "section"), None),
        P(("groups", "section"), None),
        P(None, None, "section"),
        P("section", None),
        P("groups", None, "section"),
        P(),
        P("groups", None, None),
        P("groups", None),
        P(),
        P(),
        P(),
    )
    out_specs = (P(("groups", "section"), None), P(("groups", "section"), None))
    sections = mesh.shape["section"] // GROUP
    return jax.shard_map(
        functools.partial(body, sections), mesh=mesh, in_specs=in_specs, out_specs=out_specs,
        check_vma=False,
    )
```

```python
import functools
import math

import jax
import jax.numpy as jnp
from jax import lax
from jax.experimental import pallas as pl
from jax.experimental.pallas import tpu as pltpu
from jax.sharding import PartitionSpec as P

HS = 128
GROUP = 8
CHIPS = GROUP // 2
SHARES = (7, 5)
CHUNKS = len(SHARES)
EXTRA = 16
LAG = 2
EPS = 1e-06
F32 = jnp.float32
BF16 = jnp.bfloat16
MESH = pl.DeviceIdType.MESH


def wait_for(ref, sem):
    pltpu.make_async_copy(ref, ref, sem).wait()


def kernel(
    sections,
    hid, lat, wqkv, wout, kv, gain_in, mod_in, fmod_in, wfin, wemb, flow,
    hout, lout,
    X, Z, W, WO, KV, WE, WF, PF, SB, RB, CB, CR, R, ZS,
    gain, mod, fmod, LAT, EX, SW, MH, WC, QKV,
    load_sem, sib_sem, cross_sem, ag_sem, agsib_sem, relay_sem, z_sem, send_sem,
):
    ticks = flow.shape[1]
    rows, depth = hid.shape
    latents = lat.shape[1]
    lanes = 2 * latents
    width = wqkv.shape[2]
    total = kv.shape[1]
    tokens = rows * GROUP
    heads = width // HS
    unit = depth // sum(SHARES)
    steps = [share * unit for share in SHARES]
    cols = [pl.ds(sum(steps[:c]), steps[c]) for c in range(CHUNKS)]

    me = lax.axis_index("section")
    sec = me // GROUP
    pos = me % GROUP
    core = pos % 2
    chip = pos // 2
    base = sec * GROUP
    sibling = base + chip * 2 + 1 - core
    low, high = chip % 2, chip // 2
    others = [chip + 1 - 2 * low, chip + 2 - 4 * high, 3 - chip]
    order = [2, core, 1 - core]

    def other(r):
        if isinstance(r, int):
            return others[r]
        return chip + (1 - r) * (1 - 2 * low) + r * (2 - 4 * high)

    def peer(r):
        return base + other(r) * 2 + core

    first = sec == 0
    last = sec == sections - 1
    after = (me + GROUP) % (sections * GROUP)
    before = (me + (sections - 1) * GROUP) % (sections * GROUP)
    last_base = (sections - 1) * GROUP

    def remote(src, dst, send, recv, target):
        return pltpu.make_async_remote_copy(
            src_ref=src, dst_ref=dst, send_sem=send, recv_sem=recv,
            device_id={"section": target}, device_id_type=MESH,
        )

    loads = [
        pltpu.make_async_copy(hid, X.at[0, chip, core], load_sem.at[0]),
        pltpu.make_async_copy(wqkv.at[0], W.at[:, pl.ds(0, width)], load_sem.at[1]),
        pltpu.make_async_copy(wqkv.at[1], W.at[:, pl.ds(width, width)], load_sem.at[2]),
        pltpu.make_async_copy(wqkv.at[2], W.at[:, pl.ds(2 * width, width)], load_sem.at[3]),
        pltpu.make_async_copy(kv, KV, load_sem.at[4]),
        pltpu.make_async_copy(wout, WO, load_sem.at[5]),
        pltpu.make_async_copy(wemb, WE, load_sem.at[6]),
        pltpu.make_async_copy(wfin, WF, load_sem.at[7]),
        pltpu.make_async_copy(gain_in, gain, load_sem.at[8]),
        pltpu.make_async_copy(fmod_in, fmod, load_sem.at[9]),
        pltpu.make_async_copy(mod_in, mod, load_sem.at[10]),
        pltpu.make_async_copy(lat, LAT, load_sem.at[11]),
    ]
    for load in loads:
        load.start()

    barrier = pltpu.get_barrier_semaphore()

    def greet(target):
        pl.semaphore_signal(barrier, inc=1, device_id={"section": target}, device_id_type=MESH)

    greet(sibling)
    for r in range(CHIPS - 1):
        greet(peer(r))

    @pl.when(first)
    def _():
        for i in range(GROUP):
            greet(last_base + i)

    @pl.when(last)
    def _():
        for i in range(GROUP):
            greet(i)

    if sections > 2:

        @pl.when(jnp.logical_not(last))
        def _():
            greet(after)

        @pl.when(jnp.logical_not(first))
        def _():
            greet(before)

    if sections == 2:
        pl.semaphore_wait(barrier, CHIPS + GROUP)
    else:
        edge = jnp.logical_or(first, last)

        @pl.when(edge)
        def _():
            pl.semaphore_wait(barrier, CHIPS + GROUP + 1)

        @pl.when(jnp.logical_not(edge))
        def _():
            pl.semaphore_wait(barrier, CHIPS + 2)

    def split(v):
        high_part = v.astype(BF16)
        return high_part, (v - high_part.astype(F32)).astype(BF16)

    def param(k, c):
        return mod[k, pl.ds(sec, 1), cols[c]]

    def extra_rows(scale, shift):
        row = lax.broadcasted_iota(jnp.int32, (EXTRA, scale.shape[1]), 0)
        block = jnp.zeros((EXTRA, scale.shape[1]), F32)
        for k, v in enumerate(split(scale) + split(shift)):
            block = jnp.where(row == k, v.astype(F32), block)
        return block.astype(BF16)

    def accumulate(x, scale, extra, times, state):
        if state is None:
            start = jnp.mean(x, axis=-1, keepdims=True)
        else:
            start = state[0]
        d = x - start
        s1 = jnp.sum(d, axis=-1, keepdims=True)
        s2 = jnp.sum(d * d, axis=-1, keepdims=True)
        raw = times(jnp.concatenate([(d * scale).astype(BF16), extra], axis=0))
        if state is None:
            return start, s1, s2, raw
        return start, state[1] + s1, state[2] + s2, state[3] + raw

    def finish(state):
        start, s1, s2, raw = state
        count = start.shape[0]
        rest = s1 / depth
        inverse = lax.rsqrt(jnp.maximum(s2 / depth - rest * rest, 0.0) + EPS)
        scale_sums = raw[count : count + 1] + raw[count + 1 : count + 2]
        shift_sums = raw[count + 2 : count + 3] + raw[count + 3 : count + 4]
        return inverse * (raw[:count] - rest * scale_sums) + shift_sums, shift_sums

    def prepare():
        ZS[...] = jnp.zeros_like(ZS)
        Z[0, pos] = jnp.zeros((rows, lanes), BF16)
        loads[11].wait()
        Z[0, pos, :, 0:latents] = LAT[...]
        loads[10].wait()
        for c in range(CHUNKS):
            EX[:, cols[c]] = extra_rows(1.0 + param(1, c), param(0, c))

    loads[0].wait()

    def embed(z, c):
        return jnp.dot(z, WE[:, cols[c]], preferred_element_type=F32).astype(BF16)

    def gather(t):
        def forward(c):
            wait_for(X.at[t, pl.ds(0, CHIPS - 1), 0, :, cols[c]], ag_sem.at[c])
            blocks = X.at[t, :, core, :, cols[c]]
            remote(blocks, blocks, send_sem.at[5], agsib_sem.at[c], sibling).start()

        def multiply(c, state):
            wait_for(X.at[t, :, 0, :, cols[c]], agsib_sem.at[c])
            x = X[t, :, :, :, cols[c]].reshape(tokens, steps[c]).astype(F32)

            def times(y):
                return jnp.dot(y, W[cols[c], :], preferred_element_type=F32)

            return accumulate(x, 1.0 + param(1, c), EX[:, cols[c]], times, state)

        state = None
        for c in range(CHUNKS):

            @pl.when(t > 0)
            def _():
                wait_for(X.at[t, chip, core, :, cols[c]], relay_sem.at[t, c])

            block = X.at[t, chip, core, :, cols[c]]
            for r in order:
                remote(block, block, send_sem.at[0], ag_sem.at[c], peer(r)).start()
            if c == 0:

                @pl.when(t == 0)
                def _():
                    prepare()

            if c > 0:
                forward(c - 1)
            if c == 1:

                @pl.when(t == 0)
                def _():
                    for load in loads[1:10]:
                        load.wait()

            if c > 1:
                state = multiply(c - 2, state)
        state = multiply(CHUNKS - 2, state)
        forward(CHUNKS - 1)
        values, shift_sums = finish(multiply(CHUNKS - 1, state))
        SW[0:1, :] = shift_sums
        QKV[...] = values
        wait_for(X.at[t, pl.ds(0, CHIPS - 1), 0], send_sem.at[0])
        wait_for(X.at[t, :, 0], send_sem.at[5])

    def fold():
        centre = jnp.mean(WE[...].astype(F32), axis=-1, keepdims=True)
        folded = None
        for c in range(CHUNKS):
            w = WE[:, cols[c]].astype(F32) - centre
            WC[0:latents, cols[c]], WC[latents : 2 * latents, cols[c]] = split(w)
            term = jnp.dot(
                (w * (1.0 + param(1, c))).astype(BF16), W[cols[c], :], preferred_element_type=F32
            )
            folded = term if folded is None else folded + term
        MH[0:latents, :], MH[latents : 2 * latents, :] = split(folded)

    def embedded(t):
        z = Z[t].reshape(tokens, lanes)[:, : 2 * latents]
        squares = None
        for c in range(CHUNKS):
            h = jnp.dot(z, WC[:, cols[c]], preferred_element_type=F32)
            term = jnp.sum(h * h, axis=-1, keepdims=True)
            squares = term if squares is None else squares + term
        inverse = lax.rsqrt(squares / depth + EPS)
        QKV[...] = inverse * jnp.dot(z, MH[...], preferred_element_type=F32) + SW[0:1, :]

    def tick(t, carry):
        par = t % 2

        @pl.when(jnp.logical_and(t > 0, first))
        def _():
            wait_for(Z.at[t], z_sem.at[t])
            embedded(t)

        @pl.when(jnp.logical_and(t > 0, jnp.logical_not(first)))
        def _():
            wait_for(Z.at[t, pos], z_sem.at[t])

        @pl.when(jnp.logical_or(t == 0, jnp.logical_not(first)))
        def _():
            gather(t)

        qkv = QKV[...]

        def head_norm(v, g):
            return (
                v * lax.rsqrt(jnp.mean(v * v, axis=-1, keepdims=True) + EPS) * g
            ).astype(BF16)

        patch = flow[sec, t]
        outs = []
        for h in range(heads):
            at = slice(h * HS, (h + 1) * HS)
            qn = head_norm(qkv[:, at], gain[sec, 0:1, :])
            kn = head_norm(qkv[:, width + h * HS : width + (h + 1) * HS], gain[sec, 1:2, :])
            vb = qkv[:, 2 * width + h * HS : 2 * width + (h + 1) * HS].astype(BF16)
            for which, fresh in ((0, kn), (1, vb)):
                for j in range(total // tokens):
                    place = slice(j * tokens, (j + 1) * tokens)
                    KV[which, place, at] = jnp.where(
                        patch == j, fresh.astype(F32), KV[which, place, at].astype(F32)
                    ).astype(BF16)
            scores = lax.dot_general(
                qn, KV[0, :, at], (((1,), (1,)), ((), ())), preferred_element_type=F32
            ) * (1.0 / math.sqrt(HS))
            e = jnp.exp(scores)
            totals = jnp.sum(e, axis=-1, keepdims=True)
            mixed = jnp.dot(e.astype(BF16), KV[1, :, at], preferred_element_type=F32)
            outs.append((mixed / totals).astype(BF16))
        attended = jnp.concatenate(outs, axis=1)

        def project(c):
            product = jnp.dot(attended, WO[:, cols[c]], preferred_element_type=F32)
            product = product.reshape(CHIPS, 2, rows, steps[c])
            for side in range(2):
                PF[side, :, :, cols[c]] = product[:, side]
            SB[:, :, cols[c]] = PF[1 - core, :, :, cols[c]].astype(BF16)
            remote(
                SB.at[:, :, cols[c]], RB.at[par, :, :, cols[c]],
                send_sem.at[1], sib_sem.at[par, c], sibling,
            ).start()

        def share(c):
            wait_for(RB.at[par, :, :, cols[c]], sib_sem.at[par, c])
            both = PF[core, :, :, cols[c]] + RB[par, :, :, cols[c]].astype(F32)
            PF[core, :, :, cols[c]] = both
            CB[:, :, cols[c]] = both.astype(BF16)
            for r in order:
                remote(
                    CB.at[other(r), :, cols[c]], CR.at[par, r, :, cols[c]],
                    send_sem.at[2], cross_sem.at[par, c], peer(r),
                ).start()

        for c in range(CHUNKS):
            project(c)
            if c >= LAG:
                share(c - LAG)
        for c in range(CHUNKS - LAG, CHUNKS):
            share(c)

        @pl.when(jnp.logical_and(t > 0, first))
        def _():
            z = Z[t, pos][:, :latents]
            for c in range(CHUNKS):
                X[t, chip, core, :, cols[c]] = embed(z, c)

        def combine(c):
            wait_for(CR.at[par, :, :, cols[c]], cross_sem.at[par, c])
            summed = PF[core, chip, :, cols[c]]
            for r in range(CHIPS - 1):
                summed = summed + CR[par, r, :, cols[c]].astype(F32)
            result = X[t, chip, core, :, cols[c]].astype(F32) + param(2, c) * summed
            return result.astype(BF16)

        @pl.when(jnp.logical_not(last))
        def _():
            copy = remote(Z.at[t, pos], Z.at[t + 1, pos], send_sem.at[4], z_sem.at[t + 1], after)
            copy.start()
            for c in range(CHUNKS):
                R[:, cols[c]] = combine(c)
                remote(
                    R.at[:, cols[c]], X.at[t + 1, chip, core, :, cols[c]],
                    send_sem.at[3], relay_sem.at[t + 1, c], after,
                ).start()
            wait_for(Z.at[t, pos], send_sem.at[4])
            wait_for(R, send_sem.at[3])

        @pl.when(last)
        def _():
            state = None
            for c in range(CHUNKS):

                def times(y):
                    return lax.dot_general(
                        y, WF[:, cols[c]], (((1,), (1,)), ((), ())), preferred_element_type=F32
                    )

                scale = 1.0 + fmod[1:2, cols[c]]
                extra = extra_rows(scale, fmod[0:1, cols[c]])
                state = accumulate(combine(c).astype(F32), scale, extra, times, state)
            velocity, _ = finish(state)
            renewed = (Z[t, pos][:, :latents].astype(F32) + velocity).astype(BF16)
            ZS[...] = jnp.concatenate([renewed, renewed], axis=1)
            for i in range(GROUP):
                remote(ZS, Z.at[t + 1, pos], send_sem.at[4], z_sem.at[t + 1], i).start()
            wait_for(Z.at[t], send_sem.at[4])

        @pl.when(jnp.logical_and(t == 0, first))
        def _():
            fold()

        wait_for(SB, send_sem.at[1])
        wait_for(CR.at[par], send_sem.at[2])
        return carry

    lax.fori_loop(0, ticks, tick, 0)

    @pl.when(first)
    def _():
        wait_for(Z.at[ticks], z_sem.at[ticks])
        z = Z[ticks, pos][:, :latents]
        for c in range(CHUNKS):
            hout[:, cols[c]] = embed(z, c)

    @pl.when(jnp.logical_not(first))
    def _():
        wait_for(Z.at[ticks, pos], z_sem.at[ticks])
        for c in range(CHUNKS):
            wait_for(X.at[ticks, chip, core, :, cols[c]], relay_sem.at[ticks, c])
        hout[...] = X[ticks, chip, core]

    lout[...] = Z[ticks, pos][:, :latents]


def body(
    sections, hidden_in, latent_in, w_qkv, w_out, stale_kv, qk_gain, block_mod, final_mod,
    w_final, w_embed, patch_flow,
):
    rows, depth = hidden_in.shape
    latents = latent_in.shape[1]
    lanes = 2 * latents
    width = w_qkv.shape[2]
    ticks = patch_flow.shape[0]
    anywhere = pl.BlockSpec(memory_space=pltpu.HBM)
    vmem = pl.BlockSpec(memory_space=pltpu.VMEM)
    smem = pl.BlockSpec(memory_space=pltpu.SMEM)
    dma = pltpu.SemaphoreType.DMA
    macs = ticks * rows * GROUP * depth * width * 4
    return pl.pallas_call(
        functools.partial(kernel, sections),
        out_shape=(
            jax.ShapeDtypeStruct((rows, depth), BF16),
            jax.ShapeDtypeStruct((rows, latents), BF16),
        ),
        in_specs=[
            anywhere, anywhere, anywhere, anywhere, anywhere, anywhere, anywhere, anywhere,
            anywhere, anywhere, smem,
        ],
        out_specs=(vmem, vmem),
        scratch_shapes=[
            pltpu.VMEM((ticks + 1, CHIPS, 2, rows, depth), BF16),
            pltpu.VMEM((ticks + 1, GROUP, rows, lanes), BF16),
            pltpu.VMEM((depth, 3 * width), BF16),
            pltpu.VMEM((width, depth), BF16),
            pltpu.VMEM(stale_kv.shape, BF16),
            pltpu.VMEM(w_embed.shape, BF16),
            pltpu.VMEM((latents, depth), BF16),
            pltpu.VMEM((2, CHIPS, rows, depth), F32),
            pltpu.VMEM((CHIPS, rows, depth), BF16),
            pltpu.VMEM((2, CHIPS, rows, depth), BF16),
            pltpu.VMEM((CHIPS, rows, depth), BF16),
            pltpu.VMEM((2, CHIPS - 1, rows, depth), BF16),
            pltpu.VMEM((rows, depth), BF16),
            pltpu.VMEM((rows, lanes), BF16),
            pltpu.VMEM(qk_gain.shape, F32),
            pltpu.VMEM((3, sections, depth), F32),
            pltpu.VMEM(final_mod.shape, F32),
            pltpu.VMEM((rows, latents), BF16),
            pltpu.VMEM((EXTRA, depth), BF16),
            pltpu.VMEM((8, 3 * width), F32),
            pltpu.VMEM((lanes, 3 * width), BF16),
            pltpu.VMEM((lanes, depth), BF16),
            pltpu.VMEM((rows * GROUP, 3 * width), F32),
            dma((12,)),
            dma((2, CHUNKS)),
            dma((2, CHUNKS)),
            dma((CHUNKS,)),
            dma((CHUNKS,)),
            dma((ticks + 1, CHUNKS)),
            dma((ticks + 1,)),
            dma((6,)),
        ],
        compiler_params=pltpu.CompilerParams(
            collective_id=0, has_side_effects=True, vmem_limit_bytes=64 * 1024 * 1024
        ),
        cost_estimate=pl.CostEstimate(flops=2 * macs, bytes_accessed=10**7, transcendentals=0),
    )(
        hidden_in, latent_in, w_qkv, w_out, stale_kv, qk_gain,
        jnp.transpose(block_mod, (1, 0, 2)), final_mod, w_final.T, w_embed, patch_flow.T,
    )


def solution(mesh):
    in_specs = (
        P(("groups", "section"), None),
        P(("groups", "section"), None),
        P(None, None, "section"),
        P("section", None),
        P("groups", None, "section"),
        P(),
        P("groups", None, None),
        P("groups", None),
        P(),
        P(),
        P(),
    )
    out_specs = (P(("groups", "section"), None), P(("groups", "section"), None))
    sections = mesh.shape["section"] // GROUP
    return jax.shard_map(
        functools.partial(body, sections), mesh=mesh, in_specs=in_specs, out_specs=out_specs,
        check_vma=False,
    )
```

```python
import functools
import math

import jax
import jax.numpy as jnp
from jax import lax
from jax.experimental import pallas as pl
from jax.experimental.pallas import tpu as pltpu
from jax.sharding import PartitionSpec as P

HS = 128
GROUP = 8
CHIPS = GROUP // 2
SHARES = (5, 4, 3)
CHUNKS = len(SHARES)
EXTRA = 16
LAG = 2
EPS = 1e-06
F32 = jnp.float32
BF16 = jnp.bfloat16
MESH = pl.DeviceIdType.MESH


def wait_for(ref, sem):
    pltpu.make_async_copy(ref, ref, sem).wait()


def kernel(
    sections,
    hid, lat, wqkv, wout, kv, gain_in, mod_in, fmod_in, wfin, wemb, flow,
    hout, lout,
    X, Z, W, WO, KV, WE, WF, PF, SB, RB, CB, CR, R, ZS,
    gain, mod, fmod, LAT, EX, SW, MH, WC, QKV,
    load_sem, sib_sem, cross_sem, ag_sem, agsib_sem, relay_sem, z_sem, send_sem,
):
    ticks = flow.shape[1]
    rows, depth = hid.shape
    latents = lat.shape[1]
    lanes = 2 * latents
    width = wqkv.shape[2]
    total = kv.shape[1]
    tokens = rows * GROUP
    heads = width // HS
    unit = depth // sum(SHARES)
    steps = [share * unit for share in SHARES]
    cols = [pl.ds(sum(steps[:c]), steps[c]) for c in range(CHUNKS)]

    me = lax.axis_index("section")
    sec = me // GROUP
    pos = me % GROUP
    core = pos % 2
    chip = pos // 2
    base = sec * GROUP
    sibling = base + chip * 2 + 1 - core
    low, high = chip % 2, chip // 2
    others = [chip + 1 - 2 * low, chip + 2 - 4 * high, 3 - chip]
    order = [2, core, 1 - core]

    def other(r):
        if isinstance(r, int):
            return others[r]
        return chip + (1 - r) * (1 - 2 * low) + r * (2 - 4 * high)

    def peer(r):
        return base + other(r) * 2 + core

    first = sec == 0
    last = sec == sections - 1
    after = (me + GROUP) % (sections * GROUP)
    before = (me + (sections - 1) * GROUP) % (sections * GROUP)
    last_base = (sections - 1) * GROUP

    def remote(src, dst, send, recv, target):
        return pltpu.make_async_remote_copy(
            src_ref=src, dst_ref=dst, send_sem=send, recv_sem=recv,
            device_id={"section": target}, device_id_type=MESH,
        )

    loads = [
        pltpu.make_async_copy(hid, X.at[0, chip, core], load_sem.at[0]),
        pltpu.make_async_copy(wqkv.at[0], W.at[:, pl.ds(0, width)], load_sem.at[1]),
        pltpu.make_async_copy(wqkv.at[1], W.at[:, pl.ds(width, width)], load_sem.at[2]),
        pltpu.make_async_copy(wqkv.at[2], W.at[:, pl.ds(2 * width, width)], load_sem.at[3]),
        pltpu.make_async_copy(kv, KV, load_sem.at[4]),
        pltpu.make_async_copy(wout, WO, load_sem.at[5]),
        pltpu.make_async_copy(wemb, WE, load_sem.at[6]),
        pltpu.make_async_copy(wfin, WF, load_sem.at[7]),
        pltpu.make_async_copy(gain_in, gain, load_sem.at[8]),
        pltpu.make_async_copy(fmod_in, fmod, load_sem.at[9]),
        pltpu.make_async_copy(mod_in, mod, load_sem.at[10]),
        pltpu.make_async_copy(lat, LAT, load_sem.at[11]),
    ]
    for load in loads:
        load.start()

    barrier = pltpu.get_barrier_semaphore()

    def greet(target):
        pl.semaphore_signal(barrier, inc=1, device_id={"section": target}, device_id_type=MESH)

    greet(sibling)
    for r in range(CHIPS - 1):
        greet(peer(r))

    @pl.when(first)
    def _():
        for i in range(GROUP):
            greet(last_base + i)

    @pl.when(last)
    def _():
        for i in range(GROUP):
            greet(i)

    if sections > 2:

        @pl.when(jnp.logical_not(last))
        def _():
            greet(after)

        @pl.when(jnp.logical_not(first))
        def _():
            greet(before)

    if sections == 2:
        pl.semaphore_wait(barrier, CHIPS + GROUP)
    else:
        edge = jnp.logical_or(first, last)

        @pl.when(edge)
        def _():
            pl.semaphore_wait(barrier, CHIPS + GROUP + 1)

        @pl.when(jnp.logical_not(edge))
        def _():
            pl.semaphore_wait(barrier, CHIPS + 2)

    def split(v):
        high_part = v.astype(BF16)
        return high_part, (v - high_part.astype(F32)).astype(BF16)

    def param(k, c):
        return mod[k, pl.ds(sec, 1), cols[c]]

    def extra_rows(scale, shift):
        row = lax.broadcasted_iota(jnp.int32, (EXTRA, scale.shape[1]), 0)
        block = jnp.zeros((EXTRA, scale.shape[1]), F32)
        for k, v in enumerate(split(scale) + split(shift)):
            block = jnp.where(row == k, v.astype(F32), block)
        return block.astype(BF16)

    def accumulate(x, scale, extra, times, state):
        if state is None:
            start = jnp.mean(x, axis=-1, keepdims=True)
        else:
            start = state[0]
        d = x - start
        s1 = jnp.sum(d, axis=-1, keepdims=True)
        s2 = jnp.sum(d * d, axis=-1, keepdims=True)
        raw = times(jnp.concatenate([(d * scale).astype(BF16), extra], axis=0))
        if state is None:
            return start, s1, s2, raw
        return start, state[1] + s1, state[2] + s2, state[3] + raw

    def finish(state):
        start, s1, s2, raw = state
        count = start.shape[0]
        rest = s1 / depth
        inverse = lax.rsqrt(jnp.maximum(s2 / depth - rest * rest, 0.0) + EPS)
        scale_sums = raw[count : count + 1] + raw[count + 1 : count + 2]
        shift_sums = raw[count + 2 : count + 3] + raw[count + 3 : count + 4]
        return inverse * (raw[:count] - rest * scale_sums) + shift_sums, shift_sums

    def prepare():
        ZS[...] = jnp.zeros_like(ZS)
        Z[0, pos] = jnp.zeros((rows, lanes), BF16)
        loads[11].wait()
        Z[0, pos, :, 0:latents] = LAT[...]
        loads[10].wait()
        for c in range(CHUNKS):
            EX[:, cols[c]] = extra_rows(1.0 + param(1, c), param(0, c))

    loads[0].wait()

    def embed(z, c):
        return jnp.dot(z, WE[:, cols[c]], preferred_element_type=F32).astype(BF16)

    def gather(t):
        def forward(c):
            for k in (0, 2):
                wait_for(X.at[t, 0, 0, :, cols[c]], ag_sem.at[k, c])
            blocks = X.at[t, :, core, :, cols[c]]
            remote(blocks, blocks, send_sem.at[5], agsib_sem.at[c], sibling).start()

        def hand_on(c):
            wait_for(X.at[t, 0, 0, :, cols[c]], ag_sem.at[1, c])
            block = X.at[t, other(1), core, :, cols[c]]
            remote(block, block, send_sem.at[0], ag_sem.at[2, c], peer(0)).start()

        def multiply(c, state):
            wait_for(X.at[t, :, 0, :, cols[c]], agsib_sem.at[c])
            x = X[t, :, :, :, cols[c]].reshape(tokens, steps[c]).astype(F32)

            def times(y):
                return jnp.dot(y, W[cols[c], :], preferred_element_type=F32)

            return accumulate(x, 1.0 + param(1, c), EX[:, cols[c]], times, state)

        state = None
        for c in range(CHUNKS):

            @pl.when(t > 0)
            def _():
                wait_for(X.at[t, chip, core, :, cols[c]], relay_sem.at[t, c])

            block = X.at[t, chip, core, :, cols[c]]
            for r in (1, 0):
                remote(block, block, send_sem.at[0], ag_sem.at[r, c], peer(r)).start()
            if c == 0:

                @pl.when(t == 0)
                def _():
                    prepare()

            if c > 0:
                hand_on(c - 1)
            if c == 1:

                @pl.when(t == 0)
                def _():
                    for load in loads[1:10]:
                        load.wait()

            if c > 1:
                forward(c - 2)
        hand_on(CHUNKS - 1)
        forward(CHUNKS - 2)
        for c in range(CHUNKS - 2):
            state = multiply(c, state)
        forward(CHUNKS - 1)
        state = multiply(CHUNKS - 2, state)
        values, shift_sums = finish(multiply(CHUNKS - 1, state))
        SW[0:1, :] = shift_sums
        QKV[...] = values
        wait_for(X.at[t, pl.ds(0, CHIPS - 1), 0], send_sem.at[0])
        wait_for(X.at[t, :, 0], send_sem.at[5])

    def fold():
        centre = jnp.mean(WE[...].astype(F32), axis=-1, keepdims=True)
        folded = None
        for c in range(CHUNKS):
            w = WE[:, cols[c]].astype(F32) - centre
            WC[0:latents, cols[c]], WC[latents : 2 * latents, cols[c]] = split(w)
            term = jnp.dot(
                (w * (1.0 + param(1, c))).astype(BF16), W[cols[c], :], preferred_element_type=F32
            )
            folded = term if folded is None else folded + term
        MH[0:latents, :], MH[latents : 2 * latents, :] = split(folded)

    def embedded(t):
        z = Z[t].reshape(tokens, lanes)[:, : 2 * latents]
        squares = None
        for c in range(CHUNKS):
            h = jnp.dot(z, WC[:, cols[c]], preferred_element_type=F32)
            term = jnp.sum(h * h, axis=-1, keepdims=True)
            squares = term if squares is None else squares + term
        inverse = lax.rsqrt(squares / depth + EPS)
        QKV[...] = inverse * jnp.dot(z, MH[...], preferred_element_type=F32) + SW[0:1, :]

    def tick(t, carry):
        par = t % 2

        @pl.when(jnp.logical_and(t > 0, first))
        def _():
            wait_for(Z.at[t], z_sem.at[t])
            embedded(t)

        @pl.when(jnp.logical_and(t > 0, jnp.logical_not(first)))
        def _():
            wait_for(Z.at[t, pos], z_sem.at[t])

        @pl.when(jnp.logical_or(t == 0, jnp.logical_not(first)))
        def _():
            gather(t)

        qkv = QKV[...]

        def head_norm(v, g):
            return (
                v * lax.rsqrt(jnp.mean(v * v, axis=-1, keepdims=True) + EPS) * g
            ).astype(BF16)

        patch = flow[sec, t]
        outs = []
        for h in range(heads):
            at = slice(h * HS, (h + 1) * HS)
            qn = head_norm(qkv[:, at], gain[sec, 0:1, :])
            kn = head_norm(qkv[:, width + h * HS : width + (h + 1) * HS], gain[sec, 1:2, :])
            vb = qkv[:, 2 * width + h * HS : 2 * width + (h + 1) * HS].astype(BF16)
            for which, fresh in ((0, kn), (1, vb)):
                for j in range(total // tokens):
                    place = slice(j * tokens, (j + 1) * tokens)
                    KV[which, place, at] = jnp.where(
                        patch == j, fresh.astype(F32), KV[which, place, at].astype(F32)
                    ).astype(BF16)
            scores = lax.dot_general(
                qn, KV[0, :, at], (((1,), (1,)), ((), ())), preferred_element_type=F32
            ) * (1.0 / math.sqrt(HS))
            e = jnp.exp(scores)
            totals = jnp.sum(e, axis=-1, keepdims=True)
            mixed = jnp.dot(e.astype(BF16), KV[1, :, at], preferred_element_type=F32)
            outs.append((mixed / totals).astype(BF16))
        attended = jnp.concatenate(outs, axis=1)

        def project(c):
            product = jnp.dot(attended, WO[:, cols[c]], preferred_element_type=F32)
            product = product.reshape(CHIPS, 2, rows, steps[c])
            for side in range(2):
                PF[side, :, :, cols[c]] = product[:, side]
            SB[:, :, cols[c]] = PF[1 - core, :, :, cols[c]].astype(BF16)
            remote(
                SB.at[:, :, cols[c]], RB.at[par, :, :, cols[c]],
                send_sem.at[1], sib_sem.at[par, c], sibling,
            ).start()

        def share(c):
            wait_for(RB.at[par, :, :, cols[c]], sib_sem.at[par, c])
            both = PF[core, :, :, cols[c]] + RB[par, :, :, cols[c]].astype(F32)
            PF[core, :, :, cols[c]] = both
            CB[:, :, cols[c]] = both.astype(BF16)
            for r in order:
                remote(
                    CB.at[other(r), :, cols[c]], CR.at[par, r, :, cols[c]],
                    send_sem.at[2], cross_sem.at[par, c], peer(r),
                ).start()

        for c in range(CHUNKS):
            project(c)
            if c >= LAG:
                share(c - LAG)
        for c in range(CHUNKS - LAG, CHUNKS):
            share(c)

        @pl.when(jnp.logical_and(t > 0, first))
        def _():
            z = Z[t, pos][:, :latents]
            for c in range(CHUNKS):
                X[t, chip, core, :, cols[c]] = embed(z, c)

        def combine(c):
            wait_for(CR.at[par, :, :, cols[c]], cross_sem.at[par, c])
            summed = PF[core, chip, :, cols[c]]
            for r in range(CHIPS - 1):
                summed = summed + CR[par, r, :, cols[c]].astype(F32)
            result = X[t, chip, core, :, cols[c]].astype(F32) + param(2, c) * summed
            return result.astype(BF16)

        @pl.when(jnp.logical_not(last))
        def _():
            copy = remote(Z.at[t, pos], Z.at[t + 1, pos], send_sem.at[4], z_sem.at[t + 1], after)
            copy.start()
            for c in range(CHUNKS):
                R[:, cols[c]] = combine(c)
                remote(
                    R.at[:, cols[c]], X.at[t + 1, chip, core, :, cols[c]],
                    send_sem.at[3], relay_sem.at[t + 1, c], after,
                ).start()
            wait_for(Z.at[t, pos], send_sem.at[4])
            wait_for(R, send_sem.at[3])

        @pl.when(last)
        def _():
            state = None
            for c in range(CHUNKS):

                def times(y):
                    return lax.dot_general(
                        y, WF[:, cols[c]], (((1,), (1,)), ((), ())), preferred_element_type=F32
                    )

                scale = 1.0 + fmod[1:2, cols[c]]
                extra = extra_rows(scale, fmod[0:1, cols[c]])
                state = accumulate(combine(c).astype(F32), scale, extra, times, state)
            velocity, _ = finish(state)
            renewed = (Z[t, pos][:, :latents].astype(F32) + velocity).astype(BF16)
            ZS[...] = jnp.concatenate([renewed, renewed], axis=1)
            for i in range(GROUP):
                remote(ZS, Z.at[t + 1, pos], send_sem.at[4], z_sem.at[t + 1], i).start()
            wait_for(Z.at[t], send_sem.at[4])

        @pl.when(jnp.logical_and(t == 0, first))
        def _():
            fold()

        wait_for(SB, send_sem.at[1])
        wait_for(CR.at[par], send_sem.at[2])
        return carry

    lax.fori_loop(0, ticks, tick, 0)

    @pl.when(first)
    def _():
        wait_for(Z.at[ticks], z_sem.at[ticks])
        z = Z[ticks, pos][:, :latents]
        for c in range(CHUNKS):
            hout[:, cols[c]] = embed(z, c)

    @pl.when(jnp.logical_not(first))
    def _():
        wait_for(Z.at[ticks, pos], z_sem.at[ticks])
        for c in range(CHUNKS):
            wait_for(X.at[ticks, chip, core, :, cols[c]], relay_sem.at[ticks, c])
        hout[...] = X[ticks, chip, core]

    lout[...] = Z[ticks, pos][:, :latents]


def body(
    sections, hidden_in, latent_in, w_qkv, w_out, stale_kv, qk_gain, block_mod, final_mod,
    w_final, w_embed, patch_flow,
):
    rows, depth = hidden_in.shape
    latents = latent_in.shape[1]
    lanes = 2 * latents
    width = w_qkv.shape[2]
    ticks = patch_flow.shape[0]
    anywhere = pl.BlockSpec(memory_space=pltpu.HBM)
    vmem = pl.BlockSpec(memory_space=pltpu.VMEM)
    smem = pl.BlockSpec(memory_space=pltpu.SMEM)
    dma = pltpu.SemaphoreType.DMA
    macs = ticks * rows * GROUP * depth * width * 4
    return pl.pallas_call(
        functools.partial(kernel, sections),
        out_shape=(
            jax.ShapeDtypeStruct((rows, depth), BF16),
            jax.ShapeDtypeStruct((rows, latents), BF16),
        ),
        in_specs=[
            anywhere, anywhere, anywhere, anywhere, anywhere, anywhere, anywhere, anywhere,
            anywhere, anywhere, smem,
        ],
        out_specs=(vmem, vmem),
        scratch_shapes=[
            pltpu.VMEM((ticks + 1, CHIPS, 2, rows, depth), BF16),
            pltpu.VMEM((ticks + 1, GROUP, rows, lanes), BF16),
            pltpu.VMEM((depth, 3 * width), BF16),
            pltpu.VMEM((width, depth), BF16),
            pltpu.VMEM(stale_kv.shape, BF16),
            pltpu.VMEM(w_embed.shape, BF16),
            pltpu.VMEM((latents, depth), BF16),
            pltpu.VMEM((2, CHIPS, rows, depth), F32),
            pltpu.VMEM((CHIPS, rows, depth), BF16),
            pltpu.VMEM((2, CHIPS, rows, depth), BF16),
            pltpu.VMEM((CHIPS, rows, depth), BF16),
            pltpu.VMEM((2, CHIPS - 1, rows, depth), BF16),
            pltpu.VMEM((rows, depth), BF16),
            pltpu.VMEM((rows, lanes), BF16),
            pltpu.VMEM(qk_gain.shape, F32),
            pltpu.VMEM((3, sections, depth), F32),
            pltpu.VMEM(final_mod.shape, F32),
            pltpu.VMEM((rows, latents), BF16),
            pltpu.VMEM((EXTRA, depth), BF16),
            pltpu.VMEM((8, 3 * width), F32),
            pltpu.VMEM((lanes, 3 * width), BF16),
            pltpu.VMEM((lanes, depth), BF16),
            pltpu.VMEM((rows * GROUP, 3 * width), F32),
            dma((12,)),
            dma((2, CHUNKS)),
            dma((2, CHUNKS)),
            dma((3, CHUNKS)),
            dma((CHUNKS,)),
            dma((ticks + 1, CHUNKS)),
            dma((ticks + 1,)),
            dma((6,)),
        ],
        compiler_params=pltpu.CompilerParams(
            collective_id=0, has_side_effects=True, vmem_limit_bytes=64 * 1024 * 1024
        ),
        cost_estimate=pl.CostEstimate(flops=2 * macs, bytes_accessed=10**7, transcendentals=0),
    )(
        hidden_in, latent_in, w_qkv, w_out, stale_kv, qk_gain,
        jnp.transpose(block_mod, (1, 0, 2)), final_mod, w_final.T, w_embed, patch_flow.T,
    )


def solution(mesh):
    in_specs = (
        P(("groups", "section"), None),
        P(("groups", "section"), None),
        P(None, None, "section"),
        P("section", None),
        P("groups", None, "section"),
        P(),
        P("groups", None, None),
        P("groups", None),
        P(),
        P(),
        P(),
    )
    out_specs = (P(("groups", "section"), None), P(("groups", "section"), None))
    sections = mesh.shape["section"] // GROUP
    return jax.shard_map(
        functools.partial(body, sections), mesh=mesh, in_specs=in_specs, out_specs=out_specs,
        check_vma=False,
    )
```

```python
import functools
import math

import jax
import jax.numpy as jnp
from jax import lax
from jax.experimental import pallas as pl
from jax.experimental.pallas import tpu as pltpu
from jax.sharding import PartitionSpec as P

HS = 128
GROUP = 8
CHIPS = GROUP // 2
SHARES = (5, 4, 3)
CHUNKS = len(SHARES)
EXTRA = 16
LAG = 2
EPS = 1e-06
F32 = jnp.float32
BF16 = jnp.bfloat16
MESH = pl.DeviceIdType.MESH


def wait_for(ref, sem):
    pltpu.make_async_copy(ref, ref, sem).wait()


def kernel(
    sections,
    hid, lat, wqkv, wout, kv, gain_in, mod_in, fmod_in, wfin, wemb, flow,
    hout, lout,
    X, Z, W, WO, KV, WE, WF, PF, SB, RB, CB, CR, R, ZS,
    gain, mod, fmod, LAT, EX, SW, MH, WC, QKV,
    load_sem, sib_sem, cross_sem, ag_sem, agsib_sem, relay_sem, z_sem, send_sem,
):
    ticks = flow.shape[1]
    rows, depth = hid.shape
    latents = lat.shape[1]
    lanes = 2 * latents
    width = wqkv.shape[2]
    total = kv.shape[1]
    tokens = rows * GROUP
    heads = width // HS
    unit = depth // sum(SHARES)
    steps = [share * unit for share in SHARES]
    cols = [pl.ds(sum(steps[:c]), steps[c]) for c in range(CHUNKS)]

    me = lax.axis_index("section")
    sec = me // GROUP
    pos = me % GROUP
    core = pos % 2
    chip = pos // 2
    base = sec * GROUP
    sibling = base + chip * 2 + 1 - core
    low, high = chip % 2, chip // 2
    others = [chip + 1 - 2 * low, chip + 2 - 4 * high, 3 - chip]
    order = [2, core, 1 - core]

    def other(r):
        if isinstance(r, int):
            return others[r]
        return chip + (1 - r) * (1 - 2 * low) + r * (2 - 4 * high)

    def peer(r):
        return base + other(r) * 2 + core

    first = sec == 0
    last = sec == sections - 1
    after = (me + GROUP) % (sections * GROUP)
    before = (me + (sections - 1) * GROUP) % (sections * GROUP)
    last_base = (sections - 1) * GROUP

    def facing(r):
        return base + other(r) * 2 + 1 - core

    def remote(src, dst, send, recv, target):
        return pltpu.make_async_remote_copy(
            src_ref=src, dst_ref=dst, send_sem=send, recv_sem=recv,
            device_id={"section": target}, device_id_type=MESH,
        )

    loads = [
        pltpu.make_async_copy(hid, X.at[0, chip, core], load_sem.at[0]),
        pltpu.make_async_copy(wqkv.at[0], W.at[:, pl.ds(0, width)], load_sem.at[1]),
        pltpu.make_async_copy(wqkv.at[1], W.at[:, pl.ds(width, width)], load_sem.at[2]),
        pltpu.make_async_copy(wqkv.at[2], W.at[:, pl.ds(2 * width, width)], load_sem.at[3]),
        pltpu.make_async_copy(kv, KV, load_sem.at[4]),
        pltpu.make_async_copy(wout, WO, load_sem.at[5]),
        pltpu.make_async_copy(wemb, WE, load_sem.at[6]),
        pltpu.make_async_copy(wfin, WF, load_sem.at[7]),
        pltpu.make_async_copy(gain_in, gain, load_sem.at[8]),
        pltpu.make_async_copy(fmod_in, fmod, load_sem.at[9]),
        pltpu.make_async_copy(mod_in, mod, load_sem.at[10]),
        pltpu.make_async_copy(lat, LAT, load_sem.at[11]),
    ]
    for load in loads:
        load.start()

    barrier = pltpu.get_barrier_semaphore()

    def greet(target):
        pl.semaphore_signal(barrier, inc=1, device_id={"section": target}, device_id_type=MESH)

    greet(sibling)
    for r in range(CHIPS - 1):
        greet(peer(r))
        greet(facing(r))

    @pl.when(first)
    def _():
        for i in range(GROUP):
            greet(last_base + i)

    @pl.when(last)
    def _():
        for i in range(GROUP):
            greet(i)

    if sections > 2:

        @pl.when(jnp.logical_not(last))
        def _():
            greet(after)

        @pl.when(jnp.logical_not(first))
        def _():
            greet(before)

    if sections == 2:
        pl.semaphore_wait(barrier, GROUP - 1 + GROUP)
    else:
        edge = jnp.logical_or(first, last)

        @pl.when(edge)
        def _():
            pl.semaphore_wait(barrier, GROUP - 1 + GROUP + 1)

        @pl.when(jnp.logical_not(edge))
        def _():
            pl.semaphore_wait(barrier, GROUP - 1 + 2)

    def split(v):
        high_part = v.astype(BF16)
        return high_part, (v - high_part.astype(F32)).astype(BF16)

    def param(k, c):
        return mod[k, pl.ds(sec, 1), cols[c]]

    def extra_rows(scale, shift):
        row = lax.broadcasted_iota(jnp.int32, (EXTRA, scale.shape[1]), 0)
        block = jnp.zeros((EXTRA, scale.shape[1]), F32)
        for k, v in enumerate(split(scale) + split(shift)):
            block = jnp.where(row == k, v.astype(F32), block)
        return block.astype(BF16)

    def accumulate(x, scale, extra, times, state):
        if state is None:
            start = jnp.mean(x, axis=-1, keepdims=True)
        else:
            start = state[0]
        d = x - start
        s1 = jnp.sum(d, axis=-1, keepdims=True)
        s2 = jnp.sum(d * d, axis=-1, keepdims=True)
        raw = times(jnp.concatenate([(d * scale).astype(BF16), extra], axis=0))
        if state is None:
            return start, s1, s2, raw
        return start, state[1] + s1, state[2] + s2, state[3] + raw

    def finish(state):
        start, s1, s2, raw = state
        count = start.shape[0]
        rest = s1 / depth
        inverse = lax.rsqrt(jnp.maximum(s2 / depth - rest * rest, 0.0) + EPS)
        scale_sums = raw[count : count + 1] + raw[count + 1 : count + 2]
        shift_sums = raw[count + 2 : count + 3] + raw[count + 3 : count + 4]
        return inverse * (raw[:count] - rest * scale_sums) + shift_sums, shift_sums

    def prepare():
        ZS[...] = jnp.zeros_like(ZS)
        Z[0, pos] = jnp.zeros((rows, lanes), BF16)
        loads[11].wait()
        Z[0, pos, :, 0:latents] = LAT[...]
        loads[10].wait()
        for c in range(CHUNKS):
            EX[:, cols[c]] = extra_rows(1.0 + param(1, c), param(0, c))

    loads[0].wait()

    def embed(z, c):
        return jnp.dot(z, WE[:, cols[c]], preferred_element_type=F32).astype(BF16)

    def gather(t):
        def forward(c):
            wait_for(X.at[t, pl.ds(0, CHIPS - 1), 0, :, cols[c]], ag_sem.at[c])
            if c == CHUNKS - 1:
                return
            blocks = X.at[t, :, core, :, cols[c]]
            remote(blocks, blocks, send_sem.at[5], agsib_sem.at[c], sibling).start()

        def multiply(c, state):
            wait_for(X.at[t, :, 0, :, cols[c]], agsib_sem.at[c])
            x = X[t, :, :, :, cols[c]].reshape(tokens, steps[c]).astype(F32)

            def times(y):
                return jnp.dot(y, W[cols[c], :], preferred_element_type=F32)

            return accumulate(x, 1.0 + param(1, c), EX[:, cols[c]], times, state)

        state = None
        for c in range(CHUNKS):

            @pl.when(t > 0)
            def _():
                wait_for(X.at[t, chip, core, :, cols[c]], relay_sem.at[t, c])

            block = X.at[t, chip, core, :, cols[c]]
            for r in order:
                remote(block, block, send_sem.at[0], ag_sem.at[c], peer(r)).start()
            if c == CHUNKS - 1:
                for r in order:
                    remote(block, block, send_sem.at[5], agsib_sem.at[c], facing(r)).start()
                remote(block, block, send_sem.at[5], agsib_sem.at[c], sibling).start()
            if c == 0:

                @pl.when(t == 0)
                def _():
                    prepare()

            if c > 0:
                forward(c - 1)
            if c == 1:

                @pl.when(t == 0)
                def _():
                    for load in loads[1:10]:
                        load.wait()

            if c > 1:
                state = multiply(c - 2, state)
        state = multiply(CHUNKS - 2, state)
        forward(CHUNKS - 1)
        values, shift_sums = finish(multiply(CHUNKS - 1, state))
        SW[0:1, :] = shift_sums
        QKV[...] = values
        wait_for(X.at[t, pl.ds(0, CHIPS - 1), 0], send_sem.at[0])
        wait_for(X.at[t, :, 0], send_sem.at[5])

    def fold():
        centre = jnp.mean(WE[...].astype(F32), axis=-1, keepdims=True)
        folded = None
        for c in range(CHUNKS):
            w = WE[:, cols[c]].astype(F32) - centre
            WC[0:latents, cols[c]], WC[latents : 2 * latents, cols[c]] = split(w)
            term = jnp.dot(
                (w * (1.0 + param(1, c))).astype(BF16), W[cols[c], :], preferred_element_type=F32
            )
            folded = term if folded is None else folded + term
        MH[0:latents, :], MH[latents : 2 * latents, :] = split(folded)

    def embedded(t):
        z = Z[t].reshape(tokens, lanes)[:, : 2 * latents]
        squares = None
        for c in range(CHUNKS):
            h = jnp.dot(z, WC[:, cols[c]], preferred_element_type=F32)
            term = jnp.sum(h * h, axis=-1, keepdims=True)
            squares = term if squares is None else squares + term
        inverse = lax.rsqrt(squares / depth + EPS)
        QKV[...] = inverse * jnp.dot(z, MH[...], preferred_element_type=F32) + SW[0:1, :]

    def tick(t, carry):
        par = t % 2

        @pl.when(jnp.logical_and(t > 0, first))
        def _():
            wait_for(Z.at[t], z_sem.at[t])
            embedded(t)

        @pl.when(jnp.logical_and(t > 0, jnp.logical_not(first)))
        def _():
            wait_for(Z.at[t, pos], z_sem.at[t])

        @pl.when(jnp.logical_or(t == 0, jnp.logical_not(first)))
        def _():
            gather(t)

        qkv = QKV[...]

        def head_norm(v, g):
            return (
                v * lax.rsqrt(jnp.mean(v * v, axis=-1, keepdims=True) + EPS) * g
            ).astype(BF16)

        patch = flow[sec, t]
        outs = []
        for h in range(heads):
            at = slice(h * HS, (h + 1) * HS)
            qn = head_norm(qkv[:, at], gain[sec, 0:1, :])
            kn = head_norm(qkv[:, width + h * HS : width + (h + 1) * HS], gain[sec, 1:2, :])
            vb = qkv[:, 2 * width + h * HS : 2 * width + (h + 1) * HS].astype(BF16)
            for which, fresh in ((0, kn), (1, vb)):
                for j in range(total // tokens):
                    place = slice(j * tokens, (j + 1) * tokens)
                    KV[which, place, at] = jnp.where(
                        patch == j, fresh.astype(F32), KV[which, place, at].astype(F32)
                    ).astype(BF16)
            scores = lax.dot_general(
                qn, KV[0, :, at], (((1,), (1,)), ((), ())), preferred_element_type=F32
            ) * (1.0 / math.sqrt(HS))
            e = jnp.exp(scores)
            totals = jnp.sum(e, axis=-1, keepdims=True)
            mixed = jnp.dot(e.astype(BF16), KV[1, :, at], preferred_element_type=F32)
            outs.append((mixed / totals).astype(BF16))
        attended = jnp.concatenate(outs, axis=1)

        def project(c):
            product = jnp.dot(attended, WO[:, cols[c]], preferred_element_type=F32)
            product = product.reshape(CHIPS, 2, rows, steps[c])
            for side in range(2):
                PF[side, :, :, cols[c]] = product[:, side]
            SB[:, :, cols[c]] = PF[1 - core, :, :, cols[c]].astype(BF16)
            remote(
                SB.at[:, :, cols[c]], RB.at[par, :, :, cols[c]],
                send_sem.at[1], sib_sem.at[par, c], sibling,
            ).start()

        def share(c):
            wait_for(RB.at[par, :, :, cols[c]], sib_sem.at[par, c])
            both = PF[core, :, :, cols[c]] + RB[par, :, :, cols[c]].astype(F32)
            PF[core, :, :, cols[c]] = both
            CB[:, :, cols[c]] = both.astype(BF16)
            for r in order:
                remote(
                    CB.at[other(r), :, cols[c]], CR.at[par, r, :, cols[c]],
                    send_sem.at[2], cross_sem.at[par, c], peer(r),
                ).start()

        for c in range(CHUNKS):
            project(c)
            if c >= LAG:
                share(c - LAG)
        for c in range(CHUNKS - LAG, CHUNKS):
            share(c)

        @pl.when(jnp.logical_and(t > 0, first))
        def _():
            z = Z[t, pos][:, :latents]
            for c in range(CHUNKS):
                X[t, chip, core, :, cols[c]] = embed(z, c)

        def combine(c):
            wait_for(CR.at[par, :, :, cols[c]], cross_sem.at[par, c])
            summed = PF[core, chip, :, cols[c]]
            for r in range(CHIPS - 1):
                summed = summed + CR[par, r, :, cols[c]].astype(F32)
            result = X[t, chip, core, :, cols[c]].astype(F32) + param(2, c) * summed
            return result.astype(BF16)

        @pl.when(jnp.logical_not(last))
        def _():
            copy = remote(Z.at[t, pos], Z.at[t + 1, pos], send_sem.at[4], z_sem.at[t + 1], after)
            copy.start()
            for c in range(CHUNKS):
                R[:, cols[c]] = combine(c)
                remote(
                    R.at[:, cols[c]], X.at[t + 1, chip, core, :, cols[c]],
                    send_sem.at[3], relay_sem.at[t + 1, c], after,
                ).start()
            wait_for(Z.at[t, pos], send_sem.at[4])
            wait_for(R, send_sem.at[3])

        @pl.when(last)
        def _():
            state = None
            for c in range(CHUNKS):

                def times(y):
                    return lax.dot_general(
                        y, WF[:, cols[c]], (((1,), (1,)), ((), ())), preferred_element_type=F32
                    )

                scale = 1.0 + fmod[1:2, cols[c]]
                extra = extra_rows(scale, fmod[0:1, cols[c]])
                state = accumulate(combine(c).astype(F32), scale, extra, times, state)
            velocity, _ = finish(state)
            renewed = (Z[t, pos][:, :latents].astype(F32) + velocity).astype(BF16)
            ZS[...] = jnp.concatenate([renewed, renewed], axis=1)
            for i in range(GROUP):
                remote(ZS, Z.at[t + 1, pos], send_sem.at[4], z_sem.at[t + 1], i).start()
            wait_for(Z.at[t], send_sem.at[4])

        @pl.when(jnp.logical_and(t == 0, first))
        def _():
            fold()

        wait_for(SB, send_sem.at[1])
        wait_for(CR.at[par], send_sem.at[2])
        return carry

    lax.fori_loop(0, ticks, tick, 0)

    @pl.when(first)
    def _():
        wait_for(Z.at[ticks], z_sem.at[ticks])
        z = Z[ticks, pos][:, :latents]
        for c in range(CHUNKS):
            hout[:, cols[c]] = embed(z, c)

    @pl.when(jnp.logical_not(first))
    def _():
        wait_for(Z.at[ticks, pos], z_sem.at[ticks])
        for c in range(CHUNKS):
            wait_for(X.at[ticks, chip, core, :, cols[c]], relay_sem.at[ticks, c])
        hout[...] = X[ticks, chip, core]

    lout[...] = Z[ticks, pos][:, :latents]


def body(
    sections, hidden_in, latent_in, w_qkv, w_out, stale_kv, qk_gain, block_mod, final_mod,
    w_final, w_embed, patch_flow,
):
    rows, depth = hidden_in.shape
    latents = latent_in.shape[1]
    lanes = 2 * latents
    width = w_qkv.shape[2]
    ticks = patch_flow.shape[0]
    anywhere = pl.BlockSpec(memory_space=pltpu.HBM)
    vmem = pl.BlockSpec(memory_space=pltpu.VMEM)
    smem = pl.BlockSpec(memory_space=pltpu.SMEM)
    dma = pltpu.SemaphoreType.DMA
    macs = ticks * rows * GROUP * depth * width * 4
    return pl.pallas_call(
        functools.partial(kernel, sections),
        out_shape=(
            jax.ShapeDtypeStruct((rows, depth), BF16),
            jax.ShapeDtypeStruct((rows, latents), BF16),
        ),
        in_specs=[
            anywhere, anywhere, anywhere, anywhere, anywhere, anywhere, anywhere, anywhere,
            anywhere, anywhere, smem,
        ],
        out_specs=(vmem, vmem),
        scratch_shapes=[
            pltpu.VMEM((ticks + 1, CHIPS, 2, rows, depth), BF16),
            pltpu.VMEM((ticks + 1, GROUP, rows, lanes), BF16),
            pltpu.VMEM((depth, 3 * width), BF16),
            pltpu.VMEM((width, depth), BF16),
            pltpu.VMEM(stale_kv.shape, BF16),
            pltpu.VMEM(w_embed.shape, BF16),
            pltpu.VMEM((latents, depth), BF16),
            pltpu.VMEM((2, CHIPS, rows, depth), F32),
            pltpu.VMEM((CHIPS, rows, depth), BF16),
            pltpu.VMEM((2, CHIPS, rows, depth), BF16),
            pltpu.VMEM((CHIPS, rows, depth), BF16),
            pltpu.VMEM((2, CHIPS - 1, rows, depth), BF16),
            pltpu.VMEM((rows, depth), BF16),
            pltpu.VMEM((rows, lanes), BF16),
            pltpu.VMEM(qk_gain.shape, F32),
            pltpu.VMEM((3, sections, depth), F32),
            pltpu.VMEM(final_mod.shape, F32),
            pltpu.VMEM((rows, latents), BF16),
            pltpu.VMEM((EXTRA, depth), BF16),
            pltpu.VMEM((8, 3 * width), F32),
            pltpu.VMEM((lanes, 3 * width), BF16),
            pltpu.VMEM((lanes, depth), BF16),
            pltpu.VMEM((rows * GROUP, 3 * width), F32),
            dma((12,)),
            dma((2, CHUNKS)),
            dma((2, CHUNKS)),
            dma((CHUNKS,)),
            dma((CHUNKS,)),
            dma((ticks + 1, CHUNKS)),
            dma((ticks + 1,)),
            dma((6,)),
        ],
        compiler_params=pltpu.CompilerParams(
            collective_id=0, has_side_effects=True, vmem_limit_bytes=64 * 1024 * 1024
        ),
        cost_estimate=pl.CostEstimate(flops=2 * macs, bytes_accessed=10**7, transcendentals=0),
    )(
        hidden_in, latent_in, w_qkv, w_out, stale_kv, qk_gain,
        jnp.transpose(block_mod, (1, 0, 2)), final_mod, w_final.T, w_embed, patch_flow.T,
    )


def solution(mesh):
    in_specs = (
        P(("groups", "section"), None),
        P(("groups", "section"), None),
        P(None, None, "section"),
        P("section", None),
        P("groups", None, "section"),
        P(),
        P("groups", None, None),
        P("groups", None),
        P(),
        P(),
        P(),
    )
    out_specs = (P(("groups", "section"), None), P(("groups", "section"), None))
    sections = mesh.shape["section"] // GROUP
    return jax.shard_map(
        functools.partial(body, sections), mesh=mesh, in_specs=in_specs, out_specs=out_specs,
        check_vma=False,
    )
```
